128 devices in a mesh: seq: 32 (over y_lo, z, x), chan: 4 (over y_hi, core).
Axes of the slice: x: 4, y: 4 (y_hi: 2, y_lo: 2; y = y_hi * 2 + y_lo), z: 4, core: 2. Of those that a mesh axis runs over, the one named last changes fastest.
Arguments:
- queries: bfloat16 [32768, 512], P('seq', 'chan'), may hold values from -6 to 6
- keys: bfloat16 [32768, 512], P('seq', 'chan'), may hold values from -6 to 6
- values: bfloat16 [32768, 512], P('seq', 'chan'), may hold values from -6 to 6
- cotangent: bfloat16 [32768, 512], P('seq', 'chan'), may hold values from -6 to 6
- out_weight: bfloat16 [512, 512], P('chan'), may hold values from -0.375 to 0.375
- taps: float32 [32768, 512], P('seq', 'chan'), may hold values from -1 to 1, as said below
- skip_gain: float32 [512], P('chan'), may hold values from 0.5 to 1.5
Outputs:
- out: bfloat16 [32768, 512], P('seq', 'chan')
- query_grad: bfloat16 [32768, 512], P('seq', 'chan')
- key_grad: bfloat16 [32768, 512], P('seq', 'chan')
- value_grad: bfloat16 [32768, 512], P('seq', 'chan')
- weight_grad: float32 [512, 512], P('chan')
- taps_grad: float32 [32768, 512], P('seq', 'chan')
- skip_grad: float32 [512], P('chan')
The draws below stay inside these ranges and needn't reach their ends.
Inputs may be any that keep to these rules, and one draw needn't show every extreme that they name: taps holds each channel's filter value at lags 0 to 32767.
All inputs are finite; a program needn't handle non-finite values.
Results may differ from the reference program's by a relative error of at most 0.0049.
Values may be sent and summed in bfloat16 or wider, within the bound.
A program may use at most 64 MiB of HBM per device.

```python
import math
import jax
import jax.numpy as jnp
from jax import lax

C = 512
TOKENS = 32768


def draw_taps(key, part):
    key = jax.random.fold_in(key, 11)
    shape = (TOKENS, C)
    scales = jax.random.uniform(jax.random.fold_in(key, 1), (1, C), minval=0.5, maxval=2.0)
    noise = jnp.clip(jax.random.normal(jax.random.fold_in(key, 3), shape), -4.0, 4.0)
    return (noise * scales / math.sqrt(TOKENS)).astype(jnp.float32)


def raised(entries, stream_key, source, target, shards_of, factor):
    owner, partner = [(jnp.arange(entries.shape[position]) // (entries.shape[position] // shards_of)).reshape([-1 if axis == position else 1 for axis in range(entries.ndim)]) for position in (source, target)]
    chosen = jax.random.permutation(stream_key, shards_of)[partner]
    strong = (owner == chosen) | (owner == (partner + shards_of // 2) % shards_of)
    return jnp.where(strong, factor * entries, entries)


def shard_levels(stream_key, dims, shards, smallest, high):
    factor_of, own = 1.0, jax.random.fold_in(stream_key, 6)
    for dim, parts in shards:
        steps = jnp.exp(jax.random.uniform(jax.random.fold_in(own, dim), (parts,), jnp.float32, smallest / len(shards), high / len(shards)))
        factor_of = factor_of * jnp.repeat(steps, dims[dim] // parts).reshape([-1 if axis == dim else 1 for axis in range(len(dims))])
    return factor_of


def centred(key, dims, spread, bound, cuts=(), held_as=jnp.bfloat16):
    gain = shard_levels(key, dims, cuts, -0.22, 0.18) if cuts else 1.0
    values = jax.random.normal(key, dims, jnp.float32) * spread * gain
    return jnp.minimum(jnp.maximum(values, -bound), bound).astype(held_as)


def heavy_noise(rng, shape, width, bound, cuts, heavy, kind=jnp.bfloat16):
    entries = width * jax.random.normal(rng, shape, jnp.float32)
    if cuts:
        entries = entries * shard_levels(rng, shape, cuts, -0.22, 0.18)
    return jnp.clip(raised(entries, jax.random.fold_in(rng, 3), *heavy), -bound, bound).astype(kind)


def setup_inputs(seed: int = 0) -> dict:
    seeds = jax.random.split(jax.random.key(seed), 8)
    return {
        "queries": centred(seeds[0], (TOKENS, C), 1.0, 6.0, ((0, 32), (1, 4))),
        "keys": centred(seeds[1], (TOKENS, C), 1.0, 6.0, ((0, 32), (1, 4))),
        "values": centred(seeds[2], (TOKENS, C), 1.0, 6.0, ((0, 32), (1, 4))),
        "cotangent": centred(seeds[3], (TOKENS, C), 1.0, 6.0, ((0, 32), (1, 4))),
        "out_weight": heavy_noise(seeds[4], (C, C), C ** -0.5, 0.375, ((0, 4),), (0, 1, 4, 2.0)),
        "taps": draw_taps(jax.random.fold_in(seeds[7], 71), 0),
        "skip_gain": jnp.clip(0.5 + 1.0 * jax.random.uniform(seeds[6], (C,), jnp.float32) ** shard_levels(seeds[6], (C,), ((0, 4),), -0.2, 0.2), 0.5, 1.5),
    }


def channel_lane(lane_inputs):
    queries, keys, values, back_gate, taps, skip_gain = lane_inputs
    padded_len = 2 * TOKENS
    inner = keys.astype(jnp.float32) * values.astype(jnp.float32)
    inner_spec = jnp.fft.rfft(inner, n=padded_len, axis=0)
    taps_spec = jnp.fft.rfft(taps, n=padded_len, axis=0)
    conv = jnp.fft.irfft(taps_spec * inner_spec, n=padded_len, axis=0)[:TOKENS]
    mixed = conv + skip_gain[None, :] * inner
    inner_cot = back_gate * queries.astype(jnp.float32)
    cot_spec = jnp.fft.rfft(inner_cot, n=padded_len, axis=0)
    inner_grad = jnp.fft.irfft(jnp.conj(taps_spec) * cot_spec, n=padded_len, axis=0)[:TOKENS] + skip_gain[None, :] * inner_cot
    taps_grad = jnp.fft.irfft(jnp.conj(inner_spec) * cot_spec, n=padded_len, axis=0)[:TOKENS]
    query_grad = (back_gate * mixed).astype(jnp.bfloat16)
    key_grad = (inner_grad * values.astype(jnp.float32)).astype(jnp.bfloat16)
    value_grad = (inner_grad * keys.astype(jnp.float32)).astype(jnp.bfloat16)
    skip_grad = lax.optimization_barrier(jnp.sum(inner_cot * inner, axis=0))
    return (mixed, query_grad, key_grad, value_grad, taps_grad, skip_grad)

def reference(queries, keys, values, cotangent, out_weight, taps, skip_gain):
    lane_width = min(C, 128)
    lane_count = C // lane_width
    back_gate = jnp.dot(cotangent, out_weight.T, preferred_element_type=jnp.float32)

    def split_lanes(array):
        return array.reshape(array.shape[0], lane_count, lane_width).transpose(1, 0, 2)

    def join_lanes(array):
        return array.transpose(1, 0, 2).reshape(array.shape[1], C)
    results = lax.map(channel_lane, (split_lanes(queries), split_lanes(keys), split_lanes(values), split_lanes(back_gate), split_lanes(taps), skip_gain.reshape(lane_count, lane_width)))
    mixed = join_lanes(results[0])
    gated = (queries.astype(jnp.float32) * mixed).astype(jnp.bfloat16)
    out = jnp.dot(gated, out_weight, preferred_element_type=jnp.float32).astype(jnp.bfloat16)
    scale = 1.0 / math.sqrt(TOKENS)
    weight_grad = jnp.dot(gated.T, cotangent, preferred_element_type=jnp.float32) * scale
    query_grad = join_lanes(results[1])
    key_grad = join_lanes(results[2])
    value_grad = join_lanes(results[3])
    taps_grad = join_lanes(results[4]) * scale
    skip_grad = results[5].reshape(C) * scale
    return (out, query_grad, key_grad, value_grad, weight_grad, taps_grad, skip_grad)
```

```python
import functools
import math

import jax
import jax.numpy as jnp
import numpy as np
from jax import lax
from jax.experimental import pallas as pl
from jax.experimental.pallas import tpu as pltpu
from jax.sharding import PartitionSpec as P

MESH = pl.DeviceIdType.MESH
BF16 = jnp.bfloat16
F32 = jnp.float32
LANES = 128
CHUNKS = 4


def split_table(table):
    high = table.astype(BF16)
    low = (table - high.astype(np.float64)).astype(BF16)
    return jnp.asarray(np.stack([high, low]))


def tables(rows):
    count = rows * LANES
    ids = np.arange(rows)
    lane = np.arange(LANES)
    first = 2.0 * np.pi * (((4 * ids[:, None] + 1) * ids[None, :]) % (4 * rows)) / (4 * rows)
    second = 2.0 * np.pi * ((lane[:, None] * lane[None, :]) % LANES) / LANES
    twist = 2.0 * np.pi * ((4 * ids[:, None] + 1) * lane[None, :]) / (4 * count)
    cos, sin = np.cos(second), np.sin(second)
    return (
        split_table(np.concatenate([np.cos(first), np.sin(first)], axis=0)),
        split_table(np.block([[cos, sin], [-sin, cos]])),
        split_table(np.block([[cos, -sin], [sin, cos]])),
        split_table(np.concatenate([np.cos(first).T, np.sin(first).T], axis=1) / count),
        jnp.asarray(np.stack([np.cos(twist), np.sin(twist)]), F32),
    )


def dot(left, right):
    return jnp.dot(left, right, preferred_element_type=F32)


def split(value):
    high = value.astype(BF16)
    return high, (value - high.astype(F32)).astype(BF16)


def kernel(
    n,
    keys,
    values,
    queries,
    taps,
    cot,
    weight,
    gain,
    fa_in,
    fb_in,
    gb_in,
    ga_in,
    tw_in,
    out_o,
    query_o,
    key_o,
    value_o,
    weight_o,
    taps_o,
    skip_o,
    fa,
    fb,
    gb,
    ga,
    tw,
    stage,
    first_send,
    first_recv,
    cot_send,
    cot_recv,
    conv_send,
    conv_recv,
    grad_send,
    grad_recv,
    weight_send,
    weight_recv,
    total_send,
    total_recv,
    cot_all,
    gated_all,
    columns,
    back,
    inner_cot,
    xb,
    t_high,
    t_low,
    d_high,
    d_low,
    spec_inner,
    spec_taps,
    spec_cot,
    table_sem,
    send_sem,
    recv_sem,
    chan_send,
    chan_recv,
    relay_send,
    relay_recv,
    col_send,
    col_recv,
):
    me = lax.axis_index("seq")
    lane = lax.axis_index("chan")
    core, chip = lax.rem(lane, 2), lane // 2
    twin = 2 * chip + 1 - core
    mirror = 2 * (1 - chip) + core
    corner = 2 * (1 - chip) + 1 - core
    positions = keys.shape[0]
    blocks = positions // LANES
    rows = n * blocks
    own = LANES // n
    piece = own * blocks
    window = positions * n
    scale = 1.0 / math.sqrt(window)

    barrier = pltpu.get_barrier_semaphore()

    def greet(step, carry):
        pl.semaphore_signal(
            barrier, inc=1, device_id={"seq": lax.rem(me + step, n)}, device_id_type=MESH
        )
        return carry

    for partner in (mirror, twin, corner):
        pl.semaphore_signal(barrier, inc=1, device_id={"chan": partner}, device_id_type=MESH)
    lax.fori_loop(1, n, greet, 0)

    copies = [
        pltpu.make_async_copy(src, dst, table_sem.at[i])
        for i, (src, dst) in enumerate(
            ((fa_in, fa), (fb_in, fb), (gb_in, gb), (ga_in, ga), (tw_in, tw))
        )
    ]
    for copy in copies:
        copy.start()

    def exchange(src, dst, phase, source=None):
        def step(offset, carry):
            peer = lax.rem(me + offset, n)
            pltpu.make_async_remote_copy(
                src_ref=src.at[peer] if source is None else source,
                dst_ref=dst.at[me],
                send_sem=send_sem.at[phase],
                recv_sem=recv_sem.at[phase],
                device_id={"seq": peer},
                device_id_type=MESH,
            ).start()
            return carry

        lax.fori_loop(1, n, step, 0)
        dst[me] = src[me] if source is None else source[...]

    def await_all(buf, sem):
        part = buf.at[pl.ds(0, n - 1)]
        pltpu.make_async_copy(part, part, sem).wait()

    def pack(value, dst, index):
        for b in range(blocks):
            stage[pl.ds(b, LANES, stride=blocks), :] = value(b).T
        dst[:, index] = stage[...].astype(BF16).reshape(n, piece, LANES)

    def unpack(src, index):
        stage[...] = src[:, index].astype(F32).reshape(n * piece, LANES)
        return lambda b: stage[pl.ds(b, LANES, stride=blocks), :].T

    def block(ref, b):
        return ref[b * LANES : (b + 1) * LANES, :].astype(F32)

    def gather(src, buf, phase):
        size = positions // CHUNKS
        started = []
        for k in range(CHUNKS):
            part = pl.ds(k * size, size)
            started.append(
                pltpu.make_async_remote_copy(
                    src_ref=src.at[part],
                    dst_ref=buf.at[lane, part],
                    send_sem=chan_send.at[phase, 0, k],
                    recv_sem=chan_recv.at[phase, 0, k],
                    device_id={"chan": mirror},
                    device_id_type=MESH,
                )
            )
            started[-1].start()
        near = pltpu.make_async_remote_copy(
            src_ref=src,
            dst_ref=buf.at[lane],
            send_sem=chan_send.at[phase, 1, 0],
            recv_sem=chan_recv.at[phase, 1, 0],
            device_id={"chan": twin},
            device_id_type=MESH,
        )
        near.start()
        return started, near

    def relay(buf, phase, started):
        size = positions // CHUNKS
        passed = []
        for k in range(CHUNKS):
            part = pl.ds(k * size, size)
            started[k].wait_recv()
            passed.append(
                pltpu.make_async_remote_copy(
                    src_ref=buf.at[mirror, part],
                    dst_ref=buf.at[mirror, part],
                    send_sem=relay_send.at[phase, k],
                    recv_sem=relay_recv.at[phase, k],
                    device_id={"chan": twin},
                    device_id_type=MESH,
                )
            )
            passed[-1].start()
        return passed

    pack(lambda b: block(keys, b) * block(values, b), first_send, 0)
    pl.semaphore_wait(barrier, n + 2)
    cot_started, cot_near = gather(cot, cot_all, 0)
    col_copies = []
    for k, partner in enumerate((mirror, twin, corner)):
        col_copies.append(
            pltpu.make_async_remote_copy(
                src_ref=weight.at[:, pl.ds(pl.multiple_of(partner * LANES, LANES), LANES)],
                dst_ref=columns.at[lane],
                send_sem=col_send.at[k],
                recv_sem=col_recv.at[k],
                device_id={"chan": partner},
                device_id_type=MESH,
            )
        )
        col_copies[-1].start()
    pack(lambda b: block(taps, b), first_send, 1)
    exchange(first_send, first_recv, 0)
    cot_all[lane] = cot[...]
    columns[lane] = weight[:, pl.ds(pl.multiple_of(lane * LANES, LANES), LANES)]

    cot_passed = relay(cot_all, 0, cot_started)
    cot_near.wait_recv()
    for copy in cot_passed:
        copy.wait_recv()
    for b in range(blocks):
        part = pl.ds(b * LANES, LANES)
        total = jnp.zeros((LANES, LANES), F32)
        for g in range(0, 4, 2):
            left = jnp.concatenate([cot_all[g, part], cot_all[g + 1, part]], axis=1)
            total += lax.dot_general(
                left,
                weight[:, g * LANES : (g + 2) * LANES],
                (((1,), (1,)), ((), ())),
                preferred_element_type=F32,
            )
        back[part, :] = total
        inner_cot[part, :] = total * block(queries, b)
    pack(lambda b: inner_cot[b * LANES : (b + 1) * LANES, :], cot_send, 0)
    exchange(cot_send, cot_recv, 1)

    def forward(src, index, spec):
        for pair in range(own // 2):
            x = src[:, index, 16 * pair : 16 * pair + 16, :].astype(F32)
            for half in range(2):
                xb[:, (2 * pair + half) * LANES : (2 * pair + half + 1) * LANES] = (
                    x[:, 8 * half : 8 * half + 8, :].reshape(rows, LANES).astype(BF16)
                )
        for pair in range(own // 2):
            cols = xb[:, 2 * pair * LANES : (2 * pair + 2) * LANES]
            a = dot(fa[0], cols) + dot(fa[1], cols)
            for half in range(2):
                real = a[:rows, half * LANES : (half + 1) * LANES]
                imag = a[rows:, half * LANES : (half + 1) * LANES]
                c = 2 * pair + half
                t = jnp.concatenate(
                    [real * tw[0] - imag * tw[1], real * tw[1] + imag * tw[0]], axis=1
                )
                t_high[c * rows : (c + 1) * rows, :], t_low[c * rows : (c + 1) * rows, :] = split(t)
        for c in range(own):
            part = slice(c * rows, (c + 1) * rows)
            spec[part, :] = (
                dot(t_high[part, :], fb[0]) + dot(t_high[part, :], fb[1]) + dot(t_low[part, :], fb[0])
            )

    def inverse(left, right, conjugate, dst, index):
        sign = -1.0 if conjugate else 1.0
        for c in range(own):
            part = slice(c * rows, (c + 1) * rows)
            l_real, l_imag = left[part, :LANES], sign * left[part, LANES:]
            r_real, r_imag = right[part, :LANES], right[part, LANES:]
            high, low = split(
                jnp.concatenate(
                    [l_real * r_real - l_imag * r_imag, l_real * r_imag + l_imag * r_real], axis=1
                )
            )
            y = dot(high, gb[0]) + dot(high, gb[1]) + dot(low, gb[0])
            real, imag = y[:, :LANES], y[:, LANES:]
            d_real = split(real * tw[0] + imag * tw[1])
            d_imag = split(imag * tw[0] - real * tw[1])
            cols = slice(c * LANES, (c + 1) * LANES)
            d_high[:rows, cols], d_low[:rows, cols] = d_real
            d_high[rows:, cols], d_low[rows:, cols] = d_imag
        for pair in range(own // 2):
            cols = slice(2 * pair * LANES, (2 * pair + 2) * LANES)
            y = dot(ga[0], d_high[:, cols]) + dot(ga[1], d_high[:, cols]) + dot(ga[0], d_low[:, cols])
            dst[:, index, 16 * pair : 16 * pair + 16, :] = jnp.concatenate(
                [y[:, :LANES].reshape(n, 8, LANES), y[:, LANES:].reshape(n, 8, LANES)], axis=1
            ).astype(BF16)

    for copy in copies:
        copy.wait()
    await_all(first_recv, recv_sem.at[0])
    forward(first_recv, 0, spec_inner)
    forward(first_recv, 1, spec_taps)
    inverse(spec_taps, spec_inner, False, conv_send, 0)
    exchange(conv_send, conv_recv, 2)

    await_all(cot_recv, recv_sem.at[1])
    forward(cot_recv, 0, spec_cot)
    inverse(spec_taps, spec_cot, True, grad_send, 0)
    inverse(spec_inner, spec_cot, True, grad_send, 1)
    exchange(grad_send, grad_recv, 3)

    await_all(conv_recv, recv_sem.at[2])
    conv = unpack(conv_recv, 0)
    skip = jnp.zeros((8, LANES), F32)
    for b in range(blocks):
        part = pl.ds(b * LANES, LANES)
        inner = block(keys, b) * block(values, b)
        mixed = conv(b) + gain[...] * inner
        gated_all[lane, part, :] = (block(queries, b) * mixed).astype(BF16)
        query_o[part, :] = (back[part, :] * mixed).astype(BF16)
        skip += jnp.sum((inner_cot[part, :] * inner).reshape(LANES // 8, 8, LANES), axis=0)
    gated_started, gated_near = gather(gated_all.at[lane], gated_all, 1)
    skip_high, skip_low = split(skip)
    tail = jnp.concatenate([skip_high.astype(F32), skip_low.astype(F32)], axis=0).astype(BF16)
    gated = gated_all[lane]
    share = 4 * LANES // n
    for g in range(4):
        term = lax.dot_general(
            gated, cot_all[g], (((0,), (0,)), ((), ())), preferred_element_type=F32
        ).astype(BF16)
        count = LANES // share
        weight_send[g * count : (g + 1) * count, :share, :] = term.reshape(count, share, LANES)
    weight_send[:, share:, :] = jnp.broadcast_to(tail[None], (n, 16, LANES))
    exchange(weight_send, weight_recv, 4)
    gated_passed = relay(gated_all, 1, gated_started)

    await_all(weight_recv, recv_sem.at[4])
    sums = jnp.sum(weight_recv[...].astype(F32), axis=0)
    total_send[...] = sums[:share] * scale
    exchange(None, total_recv, 5, source=total_send)
    skip_o[...] = jnp.sum(sums[share:], axis=0, keepdims=True) * scale

    await_all(grad_recv, recv_sem.at[3])
    grad = unpack(grad_recv, 0)
    for b in range(blocks):
        part = pl.ds(b * LANES, LANES)
        inner_grad = grad(b) + gain[...] * inner_cot[part, :]
        key_o[part, :] = (inner_grad * block(values, b)).astype(BF16)
        value_o[part, :] = (inner_grad * block(keys, b)).astype(BF16)
    grad = unpack(grad_recv, 1)
    for b in range(blocks):
        taps_o[pl.ds(b * LANES, LANES), :] = grad(b) * scale

    gated_near.wait_recv()
    for copy in gated_passed:
        copy.wait_recv()
    for copy in col_copies:
        copy.wait_recv()
    half = positions // 2
    for k in range(2):
        part = pl.ds(k * half, half)
        total = jnp.zeros((half, LANES), F32)
        for g in range(0, 4, 2):
            left = jnp.concatenate([gated_all[g, part], gated_all[g + 1, part]], axis=1)
            total += dot(left, columns[g : g + 2].reshape(2 * LANES, LANES))
        out_o[part, :] = total.astype(BF16)

    await_all(total_recv, recv_sem.at[5])
    for g in range(4):
        count = LANES // share
        weight_o[:, g * LANES : (g + 1) * LANES] = total_recv[
            g * count : (g + 1) * count
        ].reshape(LANES, LANES)

    for buf, phase in (
        (first_send, 0),
        (cot_send, 1),
        (conv_send, 2),
        (grad_send, 3),
        (weight_send, 4),
        (total_recv, 5),
    ):
        await_all(buf, send_sem.at[phase])
    for copy in cot_started + gated_started + cot_passed + gated_passed + col_copies:
        copy.wait_send()
    cot_near.wait_send()
    gated_near.wait_send()


def local(n, queries, keys, values, cotangent, out_weight, taps, skip_gain):
    positions = keys.shape[0]
    blocks = positions // LANES
    rows = n * blocks
    own = LANES // n
    piece = own * blocks
    share = 4 * LANES // n
    vmem = pl.BlockSpec(memory_space=pltpu.VMEM)
    anywhere = pl.BlockSpec(memory_space=pl.ANY)
    wide = jax.ShapeDtypeStruct((positions, LANES), BF16)

    def buffers(count):
        return [pltpu.VMEM((n, count, piece, LANES), BF16)] * 2

    outs = pl.pallas_call(
        functools.partial(kernel, n),
        out_shape=[
            wide,
            wide,
            wide,
            wide,
            jax.ShapeDtypeStruct((LANES, 4 * LANES), F32),
            jax.ShapeDtypeStruct((positions, LANES), F32),
            jax.ShapeDtypeStruct((1, LANES), F32),
        ],
        in_specs=[vmem] * 7 + [anywhere] * 5,
        out_specs=[vmem] * 7,
        scratch_shapes=[
            pltpu.VMEM((2, 2 * rows, rows), BF16),
            pltpu.VMEM((2, 2 * LANES, 2 * LANES), BF16),
            pltpu.VMEM((2, 2 * LANES, 2 * LANES), BF16),
            pltpu.VMEM((2, rows, 2 * rows), BF16),
            pltpu.VMEM((2, rows, LANES), F32),
            pltpu.VMEM((positions, LANES), F32),
            *buffers(2),
            *buffers(1),
            *buffers(1),
            *buffers(2),
            pltpu.VMEM((n, share + 16, LANES), BF16),
            pltpu.VMEM((n, share + 16, LANES), BF16),
            pltpu.VMEM((share, LANES), F32),
            pltpu.VMEM((n, share, LANES), F32),
            pltpu.VMEM((4, positions, LANES), BF16),
            pltpu.VMEM((4, positions, LANES), BF16),
            pltpu.VMEM((4, LANES, LANES), BF16),
            pltpu.VMEM((positions, LANES), F32),
            pltpu.VMEM((positions, LANES), F32),
            pltpu.VMEM((rows, own * LANES), BF16),
            pltpu.VMEM((own * rows, 2 * LANES), BF16),
            pltpu.VMEM((own * rows, 2 * LANES), BF16),
            pltpu.VMEM((2 * rows, own * LANES), BF16),
            pltpu.VMEM((2 * rows, own * LANES), BF16),
            pltpu.VMEM((own * rows, 2 * LANES), F32),
            pltpu.VMEM((own * rows, 2 * LANES), F32),
            pltpu.VMEM((own * rows, 2 * LANES), F32),
            pltpu.SemaphoreType.DMA((5,)),
            pltpu.SemaphoreType.DMA((6,)),
            pltpu.SemaphoreType.DMA((6,)),
            pltpu.SemaphoreType.DMA((2, 2, CHUNKS)),
            pltpu.SemaphoreType.DMA((2, 2, CHUNKS)),
            pltpu.SemaphoreType.DMA((2, CHUNKS)),
            pltpu.SemaphoreType.DMA((2, CHUNKS)),
            pltpu.SemaphoreType.DMA((3,)),
            pltpu.SemaphoreType.DMA((3,)),
        ],
        compiler_params=pltpu.CompilerParams(
            collective_id=0, has_side_effects=True, vmem_limit_bytes=48 * 1024 * 1024
        ),
        name="hyena",
    )(
        keys,
        values,
        queries,
        taps,
        cotangent,
        out_weight,
        skip_gain.reshape(1, LANES),
        *tables(rows),
    )
    return (*outs[:6], outs[6].reshape(LANES))


def solution(mesh):
    wide = P("seq", "chan")
    return jax.shard_map(
        functools.partial(local, mesh.shape["seq"]),
        mesh=mesh,
        in_specs=(wide, wide, wide, wide, P("chan", None), wide, P("chan")),
        out_specs=(wide, wide, wide, wide, P("chan", None), wide, P("chan")),
        check_vma=False,
    )
```

```python
import functools
import math

import jax
import jax.numpy as jnp
import numpy as np
from jax import lax
from jax.experimental import pallas as pl
from jax.experimental.pallas import tpu as pltpu
from jax.sharding import PartitionSpec as P

MESH = pl.DeviceIdType.MESH
BF16 = jnp.bfloat16
F32 = jnp.float32
LANES = 128
CHUNKS = 4


def split_table(table):
    high = table.astype(BF16)
    low = (table - high.astype(np.float64)).astype(BF16)
    return jnp.asarray(np.stack([high, low]))


def tables(rows):
    count = rows * LANES
    ids = np.arange(rows)
    lane = np.arange(LANES)
    first = 2.0 * np.pi * (((4 * ids[:, None] + 1) * ids[None, :]) % (4 * rows)) / (4 * rows)
    second = 2.0 * np.pi * ((lane[:, None] * lane[None, :]) % LANES) / LANES
    twist = 2.0 * np.pi * ((4 * ids[:, None] + 1) * lane[None, :]) / (4 * count)
    cos, sin = np.cos(second), np.sin(second)
    return (
        split_table(np.concatenate([np.cos(first), np.sin(first)], axis=0)),
        jnp.asarray(np.stack([np.cos(twist), np.sin(twist)]), F32),
        split_table(np.block([[cos, sin], [-sin, cos]])),
        split_table(np.block([[cos, -sin], [sin, cos]])),
        split_table(np.concatenate([np.cos(first).T, np.sin(first).T], axis=1) / count),
    )


def in_hbm(array):
    return pltpu.with_memory_space_constraint(array, pltpu.HBM)


def dot(left, right):
    return jnp.dot(left, right, preferred_element_type=F32)


def split(value):
    high = value.astype(BF16)
    return high, (value - high.astype(F32)).astype(BF16)


def kernel(
    n,
    keys_in,
    values_in,
    taps_in,
    cot_in,
    weight_in,
    queries_in,
    fa_in,
    tw_in,
    fb_in,
    gb_in,
    ga_in,
    gain_in,
    out_o,
    query_o,
    weight_o,
    skip_o,
    inner_cot,
    grad_recv,
    keys,
    values,
    taps,
    cot_all,
    weight,
    queries,
    fa,
    tw,
    fb,
    gb,
    ga,
    gain,
    stage,
    first_send,
    first_recv,
    cot_send,
    cot_recv,
    conv_send,
    conv_recv,
    grad_send,
    weight_send,
    weight_recv,
    pair_send,
    pair_recv,
    total_recv,
    gated_all,
    columns,
    back,
    xb,
    t_high,
    t_low,
    d_high,
    d_low,
    spec_inner,
    spec_taps,
    spec_cot,
    table_sem,
    send_sem,
    recv_sem,
    chan_send,
    chan_recv,
    relay_send,
    relay_recv,
    col_send,
    col_recv,
):
    me = lax.axis_index("seq")
    lane = lax.axis_index("chan")
    core, chip = lax.rem(lane, 2), lane // 2
    twin = 2 * chip + 1 - core
    mirror = 2 * (1 - chip) + core
    corner = 2 * (1 - chip) + 1 - core
    positions = keys.shape[0]
    blocks = positions // LANES
    rows = n * blocks
    own = LANES // n
    piece = own * blocks
    window = positions * n
    scale = 1.0 / math.sqrt(window)

    barrier = pltpu.get_barrier_semaphore()

    def greet(step, carry):
        pl.semaphore_signal(
            barrier, inc=1, device_id={"seq": lax.rem(me + step, n)}, device_id_type=MESH
        )
        return carry

    for partner in (mirror, twin, corner):
        pl.semaphore_signal(barrier, inc=1, device_id={"chan": partner}, device_id_type=MESH)
    lax.fori_loop(1, n, greet, 0)

    pairs = (
        (keys_in, keys),
        (values_in, values),
        (taps_in, taps),
        (cot_in, cot_all.at[lane]),
        (weight_in, weight),
        (queries_in, queries),
        (fa_in, fa),
        (tw_in, tw),
        (fb_in, fb),
        (gb_in, gb),
        (ga_in, ga),
        (gain_in, gain),
    )
    copies = [
        pltpu.make_async_copy(src, dst, table_sem.at[i]) for i, (src, dst) in enumerate(pairs)
    ]
    for copy in copies:
        copy.start()

    plane = n // 2
    here, spot = me // plane, lax.rem(me, plane)
    across = 1 - here

    def send(src, dst, phase, peer):
        pltpu.make_async_remote_copy(
            src_ref=src,
            dst_ref=dst,
            send_sem=send_sem.at[phase],
            recv_sem=recv_sem.at[phase],
            device_id={"seq": peer},
            device_id_type=MESH,
        ).start()

    def exchange(src, dst, phase, half, index=None):
        def at(ref, slot):
            return ref.at[slot] if index is None else ref.at[slot, index]

        def step(offset, carry):
            peer = half * plane + lax.rem(spot + offset, plane)
            send(at(src, peer), at(dst, me), phase, peer)
            return carry

        lax.fori_loop(1 if half is here else 0, plane, step, 0)
        if half is here:
            if index is None:
                dst[me] = src[me]
            else:
                dst[me, index] = src[me, index]

    def exchange_all(src, dst, phase, index=None):
        exchange(src, dst, phase, across, index)
        exchange(src, dst, phase, here, index)

    def await_all(buf, sems, phase, count=n - 1, index=None):
        part = buf.at[pl.ds(0, count)] if index is None else buf.at[pl.ds(0, count), index]
        pltpu.make_async_copy(part, part, sems.at[phase]).wait()

    def pack(value, dst, index):
        for b in range(blocks):
            stage[pl.ds(b, LANES, stride=blocks), :] = value(b).T
        dst[:, index] = stage[...].astype(BF16).reshape(n, piece, LANES)

    def unpack(src, index):
        stage[...] = src[:, index].astype(F32).reshape(n * piece, LANES)
        return lambda b: stage[pl.ds(b, LANES, stride=blocks), :].T

    def block(ref, b):
        return ref[b * LANES : (b + 1) * LANES, :].astype(F32)

    def gather(src, buf, phase):
        size = positions // CHUNKS
        started = []
        for k in range(CHUNKS):
            part = pl.ds(k * size, size)
            started.append(
                pltpu.make_async_remote_copy(
                    src_ref=src.at[part],
                    dst_ref=buf.at[lane, part],
                    send_sem=chan_send.at[phase, 0, k],
                    recv_sem=chan_recv.at[phase, 0, k],
                    device_id={"chan": mirror},
                    device_id_type=MESH,
                )
            )
            started[-1].start()
        near = pltpu.make_async_remote_copy(
            src_ref=src,
            dst_ref=buf.at[lane],
            send_sem=chan_send.at[phase, 1, 0],
            recv_sem=chan_recv.at[phase, 1, 0],
            device_id={"chan": twin},
            device_id_type=MESH,
        )
        near.start()
        return started, near

    def relay(buf, phase, started):
        size = positions // CHUNKS
        passed = []
        for k in range(CHUNKS):
            part = pl.ds(k * size, size)
            started[k].wait_recv()
            passed.append(
                pltpu.make_async_remote_copy(
                    src_ref=buf.at[mirror, part],
                    dst_ref=buf.at[mirror, part],
                    send_sem=relay_send.at[phase, k],
                    recv_sem=relay_recv.at[phase, k],
                    device_id={"chan": twin},
                    device_id_type=MESH,
                )
            )
            passed[-1].start()
        return passed

    def forward(src, index, spec):
        for pair in range(own // 2):
            x = src[:, index, 16 * pair : 16 * pair + 16, :].astype(F32)
            for half in range(2):
                xb[:, (2 * pair + half) * LANES : (2 * pair + half + 1) * LANES] = (
                    x[:, 8 * half : 8 * half + 8, :].reshape(rows, LANES).astype(BF16)
                )
        for pair in range(own // 2):
            cols = xb[:, 2 * pair * LANES : (2 * pair + 2) * LANES]
            a = dot(fa[0], cols) + dot(fa[1], cols)
            for half in range(2):
                real = a[:rows, half * LANES : (half + 1) * LANES]
                imag = a[rows:, half * LANES : (half + 1) * LANES]
                c = 2 * pair + half
                t = jnp.concatenate(
                    [real * tw[0] - imag * tw[1], real * tw[1] + imag * tw[0]], axis=1
                )
                t_high[c * rows : (c + 1) * rows, :], t_low[c * rows : (c + 1) * rows, :] = split(t)
        for c in range(own):
            part = slice(c * rows, (c + 1) * rows)
            spec[part, :] = (
                dot(t_high[part, :], fb[0]) + dot(t_high[part, :], fb[1]) + dot(t_low[part, :], fb[0])
            )

    def inverse(left, right, conjugate, dst, index):
        sign = -1.0 if conjugate else 1.0
        for c in range(own):
            part = slice(c * rows, (c + 1) * rows)
            l_real, l_imag = left[part, :LANES], sign * left[part, LANES:]
            r_real, r_imag = right[part, :LANES], right[part, LANES:]
            high, low = split(
                jnp.concatenate(
                    [l_real * r_real - l_imag * r_imag, l_real * r_imag + l_imag * r_real], axis=1
                )
            )
            y = dot(high, gb[0]) + dot(high, gb[1]) + dot(low, gb[0])
            real, imag = y[:, :LANES], y[:, LANES:]
            d_real = split(real * tw[0] + imag * tw[1])
            d_imag = split(imag * tw[0] - real * tw[1])
            cols = slice(c * LANES, (c + 1) * LANES)
            d_high[:rows, cols], d_low[:rows, cols] = d_real
            d_high[rows:, cols], d_low[rows:, cols] = d_imag
        for pair in range(own // 2):
            cols = slice(2 * pair * LANES, (2 * pair + 2) * LANES)
            y = dot(ga[0], d_high[:, cols]) + dot(ga[1], d_high[:, cols]) + dot(ga[0], d_low[:, cols])
            dst[:, index, 16 * pair : 16 * pair + 16, :] = jnp.concatenate(
                [y[:, :LANES].reshape(n, 8, LANES), y[:, LANES:].reshape(n, 8, LANES)], axis=1
            ).astype(BF16)

    col_copies = [
        pltpu.make_async_remote_copy(
            src_ref=weight.at[:, pl.ds(pl.multiple_of(partner * LANES, LANES), LANES)],
            dst_ref=columns.at[lane],
            send_sem=col_send.at[k],
            recv_sem=col_recv.at[k],
            device_id={"chan": partner},
            device_id_type=MESH,
        )
        for k, partner in enumerate((mirror, twin, corner))
    ]
    share = 4 * LANES // plane
    count = LANES // share
    held = {}

    def first_out():
        exchange_all(first_send, first_recv, 0)

    def cot_out():
        held["cot"], held["cot_near"] = gather(cot_in, cot_all, 0)

    def cot_relay():
        for copy in copies[3:6]:
            copy.wait()
        held["cot_passed"] = relay(cot_all, 0, held["cot"])

    def columns_out():
        for copy in col_copies:
            copy.start()
        columns[lane] = weight[:, pl.ds(pl.multiple_of(lane * LANES, LANES), LANES)]

    def cot_signal():
        held["cot_near"].wait_recv()
        for copy in held["cot_passed"]:
            copy.wait_recv()
        for b in range(blocks):
            part = pl.ds(b * LANES, LANES)
            total = jnp.zeros((LANES, LANES), F32)
            for g in range(0, 4, 2):
                left = jnp.concatenate([cot_all[g, part], cot_all[g + 1, part]], axis=1)
                total += lax.dot_general(
                    left,
                    weight[:, g * LANES : (g + 2) * LANES],
                    (((1,), (1,)), ((), ())),
                    preferred_element_type=F32,
                )
            back[part, :] = total
            inner_cot[part, :] = total * block(queries, b)
        pack(lambda b: inner_cot[b * LANES : (b + 1) * LANES, :], cot_send, 0)
        exchange_all(cot_send, cot_recv, 1)

    def conv_signal():
        for copy in copies[6:]:
            copy.wait()
        await_all(first_recv, recv_sem, 0)
        forward(first_recv, 0, spec_inner)
        forward(first_recv, 1, spec_taps)
        inverse(spec_taps, spec_inner, False, conv_send, 0)
        exchange_all(conv_send, conv_recv, 2)

    def grad_signal():
        await_all(cot_recv, recv_sem, 1)
        forward(cot_recv, 0, spec_cot)
        inverse(spec_taps, spec_cot, True, grad_send, 0)
        exchange_all(grad_send, grad_recv, 3, 0)

    def taps_signal():
        inverse(spec_inner, spec_cot, True, grad_send, 1)
        exchange_all(grad_send, grad_recv, 4, 1)

    def gate():
        await_all(conv_recv, recv_sem, 2)
        conv = unpack(conv_recv, 0)
        skip = jnp.zeros((8, LANES), F32)
        for b in range(blocks):
            part = pl.ds(b * LANES, LANES)
            inner = block(keys, b) * block(values, b)
            mixed = conv(b) + gain[...] * inner
            gated_all[lane, part, :] = (block(queries, b) * mixed).astype(BF16)
            query_o[part, :] = (back[part, :] * mixed).astype(BF16)
            skip += jnp.sum((inner_cot[part, :] * inner).reshape(LANES // 8, 8, LANES), axis=0)
        held["gated"], held["gated_near"] = gather(gated_all.at[lane], gated_all, 1)
        held["skip"] = skip

    def weight_out():
        skip_high, skip_low = split(held["skip"])
        tail = jnp.concatenate([skip_high.astype(F32), skip_low.astype(F32)], axis=0).astype(BF16)
        gated = gated_all[lane]
        for g in range(4):
            term = lax.dot_general(
                gated, cot_all[g], (((0,), (0,)), ((), ())), preferred_element_type=F32
            ).astype(BF16)
            weight_send[g * count : (g + 1) * count, :share, :] = term.reshape(count, share, LANES)
        weight_send[:, share:, :] = jnp.broadcast_to(tail[None], (plane, 16, LANES))

        def spread(offset, carry):
            place = lax.rem(spot + offset, plane)
            send(weight_send.at[place], weight_recv.at[spot], 5, here * plane + place)
            return carry

        lax.fori_loop(1, plane, spread, 0)
        weight_recv[spot] = weight_send[spot]

    def weight_pair():
        await_all(weight_recv, recv_sem, 5, plane - 1)
        sums = jnp.sum(weight_recv[...].astype(F32), axis=0)
        pair_send[:share, :] = sums[:share]
        pair_send[share:, :] = sums[share : share + 8] + sums[share + 8 :]
        send(pair_send, pair_recv, 6, across * plane + spot)

    def weight_total():
        pltpu.make_async_copy(pair_recv, pair_recv, recv_sem.at[6]).wait()
        sums = (pair_send[...] + pair_recv[...]) * scale
        total_recv[spot] = sums[:share]
        skip_o[...] = jnp.sum(sums[share:], axis=0, keepdims=True)

        def collect(offset, carry):
            place = lax.rem(spot + offset, plane)
            send(total_recv.at[spot], total_recv.at[spot], 7, here * plane + place)
            return carry

        lax.fori_loop(1, plane, collect, 0)

    def gated_relay():
        held["gated_passed"] = relay(gated_all, 1, held["gated"])

    def project():
        held["gated_near"].wait_recv()
        for copy in held["gated_passed"] + col_copies:
            copy.wait_recv()
        half = positions // 2
        for k in range(2):
            part = pl.ds(k * half, half)
            total = jnp.zeros((half, LANES), F32)
            for g in range(0, 4, 2):
                left = jnp.concatenate([gated_all[g, part], gated_all[g + 1, part]], axis=1)
                total += dot(left, columns[g : g + 2].reshape(2 * LANES, LANES))
            out_o[part, :] = total.astype(BF16)

    def settle():
        await_all(total_recv, recv_sem, 7, plane - 1)
        for g in range(4):
            weight_o[:, g * LANES : (g + 1) * LANES] = total_recv[
                g * count : (g + 1) * count
            ].reshape(LANES, LANES)
        await_all(grad_recv, recv_sem, 3, index=0)
        await_all(grad_recv, recv_sem, 4, index=1)
        await_all(first_send, send_sem, 0)
        await_all(cot_send, send_sem, 1)
        await_all(conv_send, send_sem, 2)
        await_all(grad_send, send_sem, 3, index=0)
        await_all(grad_send, send_sem, 4, index=1)
        await_all(weight_send, send_sem, 5, plane - 1)
        pltpu.make_async_copy(pair_send, pair_send, send_sem.at[6]).wait()
        await_all(total_recv, send_sem, 7, plane - 1)
        for name in ("cot", "cot_passed", "gated", "gated_passed"):
            for copy in held[name]:
                copy.wait_send()
        for copy in col_copies + [held["cot_near"], held["gated_near"]]:
            copy.wait_send()

    copies[0].wait()
    copies[1].wait()
    pack(lambda b: block(keys, b) * block(values, b), first_send, 0)
    copies[2].wait()
    pack(lambda b: block(taps, b), first_send, 1)
    pl.semaphore_wait(barrier, n + 2)
    for step in (
        first_out,
        cot_out,
        conv_signal,
        cot_relay,
        cot_signal,
        columns_out,
        gate,
        weight_out,
        grad_signal,
        weight_pair,
        taps_signal,
        weight_total,
        gated_relay,
        project,
        settle,
    ):
        step()


def finish(
    n,
    keys_in,
    values_in,
    gain_in,
    out_i,
    query_i,
    weight_i,
    skip_i,
    inner_cot,
    grad_recv,
    out_o,
    query_o,
    key_o,
    value_o,
    weight_o,
    taps_o,
    skip_o,
    keys,
    values,
    gain,
    stage,
    key_v,
    value_v,
    taps_v,
    sem,
):
    positions = keys.shape[0]
    blocks = positions // LANES
    scale = 1.0 / math.sqrt(positions * n)
    loads = [
        pltpu.make_async_copy(src, dst, sem.at[i])
        for i, (src, dst) in enumerate(((keys_in, keys), (values_in, values), (gain_in, gain)))
    ]
    stores = [
        pltpu.make_async_copy(src, dst, sem.at[3 + i])
        for i, (src, dst) in enumerate(
            (
                (out_i, out_o),
                (query_i, query_o),
                (weight_i, weight_o),
                (skip_i, skip_o),
                (taps_v, taps_o),
                (key_v, key_o),
                (value_v, value_o),
            )
        )
    ]
    for copy in loads + stores[:4]:
        copy.start()

    def unpack(index):
        stage[...] = grad_recv[:, index].astype(F32).reshape(positions, LANES)
        return lambda b: stage[pl.ds(b, LANES, stride=blocks), :].T

    grad = unpack(1)
    for b in range(blocks):
        taps_v[pl.ds(b * LANES, LANES), :] = grad(b) * scale
    stores[4].start()
    for copy in loads:
        copy.wait()
    grad = unpack(0)
    for b in range(blocks):
        part = pl.ds(b * LANES, LANES)
        inner_grad = grad(b) + gain[...] * inner_cot[part, :]
        key_v[part, :] = (inner_grad * values[part, :].astype(F32)).astype(BF16)
        value_v[part, :] = (inner_grad * keys[part, :].astype(F32)).astype(BF16)
    stores[5].start()
    stores[6].start()
    for copy in stores:
        copy.wait()


def local(n, queries, keys, values, cotangent, out_weight, taps, skip_gain):
    positions = keys.shape[0]
    blocks = positions // LANES
    rows = n * blocks
    own = LANES // n
    piece = own * blocks
    plane = n // 2
    share = 4 * LANES // plane
    vmem = pl.BlockSpec(memory_space=pltpu.VMEM)
    far = pl.BlockSpec(memory_space=pltpu.HBM)
    wide = jax.ShapeDtypeStruct((positions, LANES), BF16)
    wide_f32 = jax.ShapeDtypeStruct((positions, LANES), F32)
    square = jax.ShapeDtypeStruct((LANES, 4 * LANES), F32)
    line = jax.ShapeDtypeStruct((1, LANES), F32)
    gain = skip_gain.reshape(1, LANES)

    def buffer(count):
        return pltpu.VMEM((n, count, piece, LANES), BF16)

    first = pl.pallas_call(
        functools.partial(kernel, n),
        out_shape=[
            wide,
            wide,
            square,
            line,
            wide_f32,
            jax.ShapeDtypeStruct((n, 2, piece, LANES), BF16),
        ],
        in_specs=[far] * 12,
        out_specs=[vmem] * 6,
        scratch_shapes=[
            pltpu.VMEM((positions, LANES), BF16),
            pltpu.VMEM((positions, LANES), BF16),
            pltpu.VMEM((positions, LANES), F32),
            pltpu.VMEM((4, positions, LANES), BF16),
            pltpu.VMEM((LANES, 4 * LANES), BF16),
            pltpu.VMEM((positions, LANES), BF16),
            pltpu.VMEM((2, 2 * rows, rows), BF16),
            pltpu.VMEM((2, rows, LANES), F32),
            pltpu.VMEM((2, 2 * LANES, 2 * LANES), BF16),
            pltpu.VMEM((2, 2 * LANES, 2 * LANES), BF16),
            pltpu.VMEM((2, rows, 2 * rows), BF16),
            pltpu.VMEM((1, LANES), F32),
            pltpu.VMEM((positions, LANES), F32),
            buffer(2),
            buffer(2),
            buffer(1),
            buffer(1),
            buffer(1),
            buffer(1),
            buffer(2),
            pltpu.VMEM((plane, share + 16, LANES), BF16),
            pltpu.VMEM((plane, share + 16, LANES), BF16),
            pltpu.VMEM((share + 8, LANES), F32),
            pltpu.VMEM((share + 8, LANES), F32),
            pltpu.VMEM((plane, share, LANES), F32),
            pltpu.VMEM((4, positions, LANES), BF16),
            pltpu.VMEM((4, LANES, LANES), BF16),
            pltpu.VMEM((positions, LANES), F32),
            pltpu.VMEM((rows, own * LANES), BF16),
            pltpu.VMEM((own * rows, 2 * LANES), BF16),
            pltpu.VMEM((own * rows, 2 * LANES), BF16),
            pltpu.VMEM((2 * rows, own * LANES), BF16),
            pltpu.VMEM((2 * rows, own * LANES), BF16),
            pltpu.VMEM((own * rows, 2 * LANES), F32),
            pltpu.VMEM((own * rows, 2 * LANES), F32),
            pltpu.VMEM((own * rows, 2 * LANES), F32),
            pltpu.SemaphoreType.DMA((12,)),
            pltpu.SemaphoreType.DMA((8,)),
            pltpu.SemaphoreType.DMA((8,)),
            pltpu.SemaphoreType.DMA((2, 2, CHUNKS)),
            pltpu.SemaphoreType.DMA((2, 2, CHUNKS)),
            pltpu.SemaphoreType.DMA((2, CHUNKS)),
            pltpu.SemaphoreType.DMA((2, CHUNKS)),
            pltpu.SemaphoreType.DMA((3,)),
            pltpu.SemaphoreType.DMA((3,)),
        ],
        compiler_params=pltpu.CompilerParams(
            collective_id=0, has_side_effects=True, vmem_limit_bytes=40 * 1024 * 1024
        ),
        name="hyena",
    )(*map(in_hbm, (keys, values, taps, cotangent, out_weight, queries, *tables(rows), gain)))
    outs = pl.pallas_call(
        functools.partial(finish, n),
        out_shape=[wide, wide, wide, wide, square, wide_f32, line],
        in_specs=[far] * 3 + [vmem] * 6,
        out_specs=[far] * 7,
        scratch_shapes=[
            pltpu.VMEM((positions, LANES), BF16),
            pltpu.VMEM((positions, LANES), BF16),
            pltpu.VMEM((1, LANES), F32),
            pltpu.VMEM((positions, LANES), F32),
            pltpu.VMEM((positions, LANES), BF16),
            pltpu.VMEM((positions, LANES), BF16),
            pltpu.VMEM((positions, LANES), F32),
            pltpu.SemaphoreType.DMA((10,)),
        ],
        compiler_params=pltpu.CompilerParams(vmem_limit_bytes=24 * 1024 * 1024),
        name="finish",
    )(*map(in_hbm, (keys, values, gain)), *first)
    return (*outs[:6], outs[6].reshape(LANES))


def solution(mesh):
    wide = P("seq", "chan")
    return jax.shard_map(
        functools.partial(local, mesh.shape["seq"]),
        mesh=mesh,
        in_specs=(wide, wide, wide, wide, P("chan", None), wide, P("chan")),
        out_specs=(wide, wide, wide, wide, P("chan", None), wide, P("chan")),
        check_vma=False,
    )
```

```python
import functools
import math

import jax
import jax.numpy as jnp
import numpy as np
from jax import lax
from jax.experimental import pallas as pl
from jax.experimental.pallas import tpu as pltpu
from jax.sharding import PartitionSpec as P

MESH = pl.DeviceIdType.MESH
BF16 = jnp.bfloat16
F32 = jnp.float32
LANES = 128
CHUNKS = 4
RING = 4


def split_table(table):
    high = table.astype(BF16)
    low = (table - high.astype(np.float64)).astype(BF16)
    return jnp.asarray(np.stack([high, low]))


def tables(rows):
    count = rows * LANES
    ids = np.arange(rows)
    lane = np.arange(LANES)
    first = 2.0 * np.pi * (((4 * ids[:, None] + 1) * ids[None, :]) % (4 * rows)) / (4 * rows)
    second = 2.0 * np.pi * ((lane[:, None] * lane[None, :]) % LANES) / LANES
    twist = 2.0 * np.pi * ((4 * ids[:, None] + 1) * lane[None, :]) / (4 * count)
    cos, sin = np.cos(second), np.sin(second)
    return (
        split_table(np.concatenate([np.cos(first), np.sin(first)], axis=0)),
        jnp.asarray(np.stack([np.cos(twist), np.sin(twist)]), F32),
        split_table(np.block([[cos, sin], [-sin, cos]])),
        split_table(np.block([[cos, -sin], [sin, cos]])),
        split_table(np.concatenate([np.cos(first).T, np.sin(first).T], axis=1) / count),
    )


def in_hbm(array):
    return pltpu.with_memory_space_constraint(array, pltpu.HBM)


def dot(left, right):
    return jnp.dot(left, right, preferred_element_type=F32)


def split(value):
    high = value.astype(BF16)
    return high, (value - high.astype(F32)).astype(BF16)


def kernel(
    n,
    keys_in,
    values_in,
    taps_in,
    cot_in,
    weight_in,
    queries_in,
    fa_in,
    tw_in,
    fb_in,
    gb_in,
    ga_in,
    gain_in,
    out_o,
    query_o,
    key_o,
    value_o,
    weight_o,
    taps_o,
    skip_o,
    inner_cot,
    grad_recv,
    keys,
    values,
    taps,
    cot_all,
    weight,
    queries,
    fa,
    tw,
    fb,
    gb,
    ga,
    gain,
    stage,
    first_send,
    first_recv,
    cot_send,
    cot_recv,
    conv_send,
    conv_recv,
    grad_send,
    weight_send,
    weight_recv,
    pair_send,
    pair_recv,
    total_recv,
    gated_all,
    columns,
    back,
    mixed_all,
    xb,
    t_high,
    t_low,
    d_high,
    d_low,
    spec_inner,
    spec_taps,
    spec_cot,
    table_sem,
    send_sem,
    recv_sem,
    chan_send,
    chan_recv,
    relay_send,
    relay_recv,
    col_send,
    col_recv,
):
    me = lax.axis_index("seq")
    lane = lax.axis_index("chan")
    core, chip = lax.rem(lane, 2), lane // 2
    twin = 2 * chip + 1 - core
    mirror = 2 * (1 - chip) + core
    corner = 2 * (1 - chip) + 1 - core
    positions = keys.shape[0]
    blocks = positions // LANES
    rows = n * blocks
    own = LANES // n
    piece = own * blocks
    window = positions * n
    scale = 1.0 / math.sqrt(window)

    barrier = pltpu.get_barrier_semaphore()

    def greet(step, carry):
        pl.semaphore_signal(
            barrier, inc=1, device_id={"seq": lax.rem(me + step, n)}, device_id_type=MESH
        )
        return carry

    for partner in (mirror, twin, corner):
        pl.semaphore_signal(barrier, inc=1, device_id={"chan": partner}, device_id_type=MESH)
    lax.fori_loop(1, n, greet, 0)

    pairs = (
        (keys_in, keys),
        (values_in, values),
        (taps_in, taps),
        (cot_in, cot_all.at[lane]),
        (weight_in, weight),
        (queries_in, queries),
        (fa_in, fa),
        (tw_in, tw),
        (fb_in, fb),
        (gb_in, gb),
        (ga_in, ga),
        (gain_in, gain),
    )
    copies = [
        pltpu.make_async_copy(src, dst, table_sem.at[i]) for i, (src, dst) in enumerate(pairs)
    ]
    for copy in copies:
        copy.start()

    plane = n // 2
    here, spot = me // plane, lax.rem(me, plane)
    across = 1 - here

    depth = plane // RING
    far_first = sorted(
        ((dz, dx) for dz in range(depth) for dx in range(RING)),
        key=lambda offset: -min(offset[0], depth - offset[0]) - min(offset[1], RING - offset[1]),
    )

    def place_at(offset):
        dz, dx = offset
        return lax.rem(spot // RING + dz, depth) * RING + lax.rem(spot + dx, RING)

    def send(src, dst, phase, peer):
        pltpu.make_async_remote_copy(
            src_ref=src,
            dst_ref=dst,
            send_sem=send_sem.at[phase],
            recv_sem=recv_sem.at[phase],
            device_id={"seq": peer},
            device_id_type=MESH,
        ).start()

    def exchange(src, dst, phase, half, index=None):
        def at(ref, slot):
            return ref.at[slot] if index is None else ref.at[slot, index]

        for offset in far_first:
            if half is here and offset == (0, 0):
                continue
            peer = half * plane + place_at(offset)
            send(at(src, peer), at(dst, me), phase, peer)
        if half is here:
            if index is None:
                dst[me] = src[me]
            else:
                dst[me, index] = src[me, index]

    def exchange_all(src, dst, phase, index=None):
        exchange(src, dst, phase, across, index)
        exchange(src, dst, phase, here, index)

    def await_all(buf, sems, phase, count=n - 1, index=None):
        part = buf.at[pl.ds(0, count)] if index is None else buf.at[pl.ds(0, count), index]
        pltpu.make_async_copy(part, part, sems.at[phase]).wait()

    def turn(value, b):
        stage[pl.ds(b, LANES, stride=blocks), :] = value.T

    def pack(value, dst, index):
        for b in range(blocks):
            turn(value(b), b)
        put(dst, index)

    def put(dst, index):
        dst[:, index] = stage[...].astype(BF16).reshape(n, piece, LANES)

    def unpack(src, index):
        stage[...] = src[:, index].astype(F32).reshape(n * piece, LANES)
        return lambda b: stage[pl.ds(b, LANES, stride=blocks), :].T

    def block(ref, b):
        return ref[b * LANES : (b + 1) * LANES, :].astype(F32)

    def gather_part(src, buf, phase, k):
        size = positions // CHUNKS
        part = pl.ds(k * size, size)
        started = [
            pltpu.make_async_remote_copy(
                src_ref=src.at[part],
                dst_ref=buf.at[lane, part],
                send_sem=chan_send.at[phase, way, k],
                recv_sem=chan_recv.at[phase, way, k],
                device_id={"chan": partner},
                device_id_type=MESH,
            )
            for way, partner in enumerate((mirror, twin))
        ]
        for copy in started:
            copy.start()
        return started

    def relay(buf, phase, started, k):
        size = positions // CHUNKS
        part = pl.ds(k * size, size)
        started[k][0].wait_recv()
        passed = pltpu.make_async_remote_copy(
            src_ref=buf.at[mirror, part],
            dst_ref=buf.at[mirror, part],
            send_sem=relay_send.at[phase, k],
            recv_sem=relay_recv.at[phase, k],
            device_id={"chan": twin},
            device_id_type=MESH,
        )
        passed.start()
        return passed

    def forward(src, index, spec):
        for pair in range(own // 2):
            x = src[:, index, 16 * pair : 16 * pair + 16, :].astype(F32)
            for half in range(2):
                xb[:, (2 * pair + half) * LANES : (2 * pair + half + 1) * LANES] = (
                    x[:, 8 * half : 8 * half + 8, :].reshape(rows, LANES).astype(BF16)
                )
        for pair in range(own // 2):
            cols = xb[:, 2 * pair * LANES : (2 * pair + 2) * LANES]
            a = dot(fa[0], cols) + dot(fa[1], cols)
            for half in range(2):
                real = a[:rows, half * LANES : (half + 1) * LANES]
                imag = a[rows:, half * LANES : (half + 1) * LANES]
                c = 2 * pair + half
                t = jnp.concatenate(
                    [real * tw[0] - imag * tw[1], real * tw[1] + imag * tw[0]], axis=1
                )
                t_high[c * rows : (c + 1) * rows, :], t_low[c * rows : (c + 1) * rows, :] = split(t)
        for c in range(own):
            part = slice(c * rows, (c + 1) * rows)
            spec[part, :] = (
                dot(t_high[part, :], fb[0]) + dot(t_high[part, :], fb[1]) + dot(t_low[part, :], fb[0])
            )

    def inverse(left, right, conjugate, dst, index):
        sign = -1.0 if conjugate else 1.0
        for c in range(own):
            part = slice(c * rows, (c + 1) * rows)
            l_real, l_imag = left[part, :LANES], sign * left[part, LANES:]
            r_real, r_imag = right[part, :LANES], right[part, LANES:]
            high, low = split(
                jnp.concatenate(
                    [l_real * r_real - l_imag * r_imag, l_real * r_imag + l_imag * r_real], axis=1
                )
            )
            y = dot(high, gb[0]) + dot(high, gb[1]) + dot(low, gb[0])
            real, imag = y[:, :LANES], y[:, LANES:]
            d_real = split(real * tw[0] + imag * tw[1])
            d_imag = split(imag * tw[0] - real * tw[1])
            cols = slice(c * LANES, (c + 1) * LANES)
            d_high[:rows, cols], d_low[:rows, cols] = d_real
            d_high[rows:, cols], d_low[rows:, cols] = d_imag
        for pair in range(own // 2):
            cols = slice(2 * pair * LANES, (2 * pair + 2) * LANES)
            y = dot(ga[0], d_high[:, cols]) + dot(ga[1], d_high[:, cols]) + dot(ga[0], d_low[:, cols])
            dst[:, index, 16 * pair : 16 * pair + 16, :] = jnp.concatenate(
                [y[:, :LANES].reshape(n, 8, LANES), y[:, LANES:].reshape(n, 8, LANES)], axis=1
            ).astype(BF16)

    team = min(8, plane)
    first_spot, rank = spot // team * team, lax.rem(spot, team)
    height = LANES // team
    mine = pl.ds(pl.multiple_of(rank * height, height), height)
    col_copies = []
    for k, partner in enumerate((mirror, corner, twin)):
        cols = pl.ds(pl.multiple_of(partner * LANES, LANES), LANES)
        part = mine if k < 2 else pl.ds(0, LANES)
        col_copies.append(
            pltpu.make_async_remote_copy(
                src_ref=weight.at[part, cols],
                dst_ref=columns.at[lane, part],
                send_sem=col_send.at[k],
                recv_sem=col_recv.at[k],
                device_id={"chan": partner},
                device_id_type=MESH,
            )
        )
    share = 4 * LANES // plane
    count = LANES // share
    held = {}

    def inner_out():
        exchange_all(first_send, first_recv, 0, 0)

    def taps_out():
        copies[2].wait()
        pack(lambda b: block(taps, b), first_send, 1)
        exchange_all(first_send, first_recv, 8, 1)

    def signals_left():
        await_all(first_send, send_sem, 0, index=0)
        await_all(first_send, send_sem, 8, index=1)

    def cot_out():
        held["cot"] = [gather_part(cot_in, cot_all, 0, k) for k in range(CHUNKS)]

    def columns_out():
        copies[4].wait()
        for copy in col_copies:
            copy.start()
        columns[lane] = weight[:, pl.ds(pl.multiple_of(lane * LANES, LANES), LANES)]

    def columns_on():
        for k, origin in enumerate((mirror, corner)):
            col_copies[k].wait_recv()
            part = columns.at[origin, mine]
            for step in range(1, team):
                peer = here * plane + first_spot + lax.rem(rank + step, team)
                send(part, part, 9 + k, peer)

    def cot_signal():
        copies[3].wait()
        copies[5].wait()
        held["cot_passed"] = []
        for k in range(CHUNKS + 1):
            if k < CHUNKS:
                held["cot_passed"].append(relay(cot_all, 0, held["cot"], k))
            if k == 0:
                continue
            held["cot"][k - 1][1].wait_recv()
            held["cot_passed"][k - 1].wait_recv()
            size = blocks // CHUNKS
            for b in range((k - 1) * size, k * size):
                part = pl.ds(b * LANES, LANES)
                total = jnp.zeros((LANES, LANES), F32)
                for g in range(0, 4, 2):
                    left = jnp.concatenate([cot_all[g, part], cot_all[g + 1, part]], axis=1)
                    total += lax.dot_general(
                        left,
                        weight[:, g * LANES : (g + 2) * LANES],
                        (((1,), (1,)), ((), ())),
                        preferred_element_type=F32,
                    )
                back[part, :] = total
                signal = total * block(queries, b)
                inner_cot[part, :] = signal
                turn(signal, b)
        put(cot_send, 0)
        exchange_all(cot_send, cot_recv, 1)

    def conv_signal():
        for copy in copies[6:]:
            copy.wait()
        await_all(first_recv, recv_sem, 0, index=0)
        forward(first_recv, 0, spec_inner)
        await_all(first_recv, recv_sem, 8, index=1)
        forward(first_recv, 1, spec_taps)
        inverse(spec_taps, spec_inner, False, conv_send, 0)
        exchange_all(conv_send, conv_recv, 2)

    def grad_signal():
        await_all(cot_recv, recv_sem, 1)
        forward(cot_recv, 0, spec_cot)
        inverse(spec_taps, spec_cot, True, grad_send, 0)

    def grad_out():
        exchange_all(grad_send, grad_recv, 3, 0)

    def taps_signal():
        inverse(spec_inner, spec_cot, True, grad_send, 1)
        exchange(grad_send, grad_recv, 4, across, 1)

    def taps_near():
        exchange(grad_send, grad_recv, 4, here, 1)

    def gate():
        await_all(conv_recv, recv_sem, 2)
        conv = unpack(conv_recv, 0)
        held["gated"] = []
        for b in range(blocks):
            part = pl.ds(b * LANES, LANES)
            mixed = conv(b) + gain[...] * (block(keys, b) * block(values, b))
            mixed_all[part, :] = mixed
            gated_all[lane, part, :] = (block(queries, b) * mixed).astype(BF16)
            if (b + 1) % (blocks // CHUNKS) == 0:
                k = b // (blocks // CHUNKS)
                held["gated"].append(gather_part(gated_all.at[lane], gated_all, 1, k))
        skip = jnp.zeros((8, LANES), F32)
        for b in range(blocks):
            part = pl.ds(b * LANES, LANES)
            product = inner_cot[part, :] * (block(keys, b) * block(values, b))
            skip += jnp.sum(product.reshape(LANES // 8, 8, LANES), axis=0)
        held["skip"] = skip

    def query_grads():
        for b in range(blocks):
            part = pl.ds(b * LANES, LANES)
            query_o[part, :] = (back[part, :] * mixed_all[part, :]).astype(BF16)

    def weight_out():
        skip_high, skip_low = split(held["skip"])
        tail = jnp.concatenate([skip_high.astype(F32), skip_low.astype(F32)], axis=0).astype(BF16)
        gated = gated_all[lane].T
        for g in range(4):
            term = dot(gated, cot_all[g]).astype(BF16)
            weight_send[g * count : (g + 1) * count, :share, :] = term.reshape(count, share, LANES)
        weight_send[:, share:, :] = jnp.broadcast_to(tail[None], (plane, 16, LANES))

        for offset in far_first[:-1]:
            place = place_at(offset)
            send(weight_send.at[place], weight_recv.at[spot], 5, here * plane + place)
        weight_recv[spot] = weight_send[spot]

    def weight_pair():
        await_all(weight_recv, recv_sem, 5, plane - 1)
        sums = jnp.sum(weight_recv[...].astype(F32), axis=0)
        pair_send[:share, :] = sums[:share]
        pair_send[share:, :] = sums[share : share + 8] + sums[share + 8 :]
        send(pair_send, pair_recv, 6, across * plane + spot)

    def weight_total():
        pltpu.make_async_copy(pair_recv, pair_recv, recv_sem.at[6]).wait()
        sums = pair_send[...] + pair_recv[...]
        total_recv[spot] = sums[:share].astype(BF16)
        skip_o[...] = jnp.sum(sums[share:], axis=0, keepdims=True) * scale

        for offset in far_first[:-1]:
            send(total_recv.at[spot], total_recv.at[spot], 7, here * plane + place_at(offset))

    def gated_relay():
        held["gated_passed"] = [relay(gated_all, 1, held["gated"], k) for k in range(CHUNKS)]

    def project():
        for copy in [pair[1] for pair in held["gated"]] + held["gated_passed"] + col_copies[2:]:
            copy.wait_recv()
        others = columns.at[0, pl.ds(0, LANES - height)]
        for phase in (9, 10):
            pltpu.make_async_copy(others, others, recv_sem.at[phase]).wait()
        half = positions // 2
        for k in range(2):
            part = pl.ds(k * half, half)
            total = jnp.zeros((half, LANES), F32)
            for g in range(0, 4, 2):
                left = jnp.concatenate([gated_all[g, part], gated_all[g + 1, part]], axis=1)
                total += dot(left, columns[g : g + 2].reshape(2 * LANES, LANES))
            out_o[part, :] = total.astype(BF16)

    def factor_grads():
        await_all(grad_recv, recv_sem, 3, index=0)
        grad = unpack(grad_recv, 0)
        for b in range(blocks):
            part = pl.ds(b * LANES, LANES)
            inner_grad = grad(b) + gain[...] * inner_cot[part, :]
            key_o[part, :] = (inner_grad * block(values, b)).astype(BF16)
            value_o[part, :] = (inner_grad * block(keys, b)).astype(BF16)

    def taps_grads():
        await_all(grad_recv, recv_sem, 4, index=1)
        grad = unpack(grad_recv, 1)
        for b in range(blocks):
            taps_o[pl.ds(b * LANES, LANES), :] = grad(b) * scale

    def settle():
        await_all(total_recv, recv_sem, 7, plane - 1)
        for g in range(4):
            weight_o[:, g * LANES : (g + 1) * LANES] = (
                total_recv[g * count : (g + 1) * count].astype(F32).reshape(LANES, LANES) * scale
            )
        await_all(cot_send, send_sem, 1)
        await_all(conv_send, send_sem, 2)
        await_all(grad_send, send_sem, 3, index=0)
        await_all(grad_send, send_sem, 4, index=1)
        await_all(weight_send, send_sem, 5, plane - 1)
        pltpu.make_async_copy(pair_send, pair_send, send_sem.at[6]).wait()
        await_all(total_recv, send_sem, 7, plane - 1)
        for name in ("cot", "gated"):
            for copy in sum(held[name], held[name + "_passed"]):
                copy.wait_send()
        others = columns.at[0, pl.ds(0, LANES - height)]
        for phase in (9, 10):
            pltpu.make_async_copy(others, others, send_sem.at[phase]).wait()
        for copy in col_copies:
            copy.wait_send()

    copies[0].wait()
    copies[1].wait()
    pack(lambda b: block(keys, b) * block(values, b), first_send, 0)
    pl.semaphore_wait(barrier, n + 2)
    for step in (
        inner_out,
        taps_out,
        cot_out,
        conv_signal,
        columns_out,
        cot_signal,
        gate,
        weight_out,
        columns_on,
        grad_signal,
        weight_pair,
        grad_out,
        taps_signal,
        taps_near,
        query_grads,
        weight_total,
        gated_relay,
        signals_left,
        project,
        factor_grads,
        taps_grads,
        settle,
    ):
        step()


def store(*refs):
    count = len(refs) // 2
    copies = [
        pltpu.make_async_copy(refs[i], refs[count + i], refs[-1].at[i]) for i in range(count)
    ]
    for copy in copies:
        copy.start()
    for copy in copies:
        copy.wait()


def local(n, queries, keys, values, cotangent, out_weight, taps, skip_gain):
    positions = keys.shape[0]
    blocks = positions // LANES
    rows = n * blocks
    own = LANES // n
    piece = own * blocks
    plane = n // 2
    share = 4 * LANES // plane
    vmem = pl.BlockSpec(memory_space=pltpu.VMEM)
    far = pl.BlockSpec(memory_space=pltpu.HBM)
    wide = jax.ShapeDtypeStruct((positions, LANES), BF16)
    wide_f32 = jax.ShapeDtypeStruct((positions, LANES), F32)
    square = jax.ShapeDtypeStruct((LANES, 4 * LANES), F32)
    line = jax.ShapeDtypeStruct((1, LANES), F32)
    gain = skip_gain.reshape(1, LANES)

    def buffer(count):
        return pltpu.VMEM((n, count, piece, LANES), BF16)

    shapes = [wide, wide, wide, wide, square, wide_f32, line]
    results = pl.pallas_call(
        functools.partial(kernel, n),
        out_shape=shapes,
        in_specs=[far] * 12,
        out_specs=[vmem] * 7,
        scratch_shapes=[
            pltpu.VMEM((positions, LANES), F32),
            buffer(2),
            pltpu.VMEM((positions, LANES), BF16),
            pltpu.VMEM((positions, LANES), BF16),
            pltpu.VMEM((positions, LANES), F32),
            pltpu.VMEM((4, positions, LANES), BF16),
            pltpu.VMEM((LANES, 4 * LANES), BF16),
            pltpu.VMEM((positions, LANES), BF16),
            pltpu.VMEM((2, 2 * rows, rows), BF16),
            pltpu.VMEM((2, rows, LANES), F32),
            pltpu.VMEM((2, 2 * LANES, 2 * LANES), BF16),
            pltpu.VMEM((2, 2 * LANES, 2 * LANES), BF16),
            pltpu.VMEM((2, rows, 2 * rows), BF16),
            pltpu.VMEM((1, LANES), F32),
            pltpu.VMEM((positions, LANES), F32),
            buffer(2),
            buffer(2),
            buffer(1),
            buffer(1),
            buffer(1),
            buffer(1),
            buffer(2),
            pltpu.VMEM((plane, share + 16, LANES), BF16),
            pltpu.VMEM((plane, share + 16, LANES), BF16),
            pltpu.VMEM((share + 8, LANES), F32),
            pltpu.VMEM((share + 8, LANES), F32),
            pltpu.VMEM((plane, share, LANES), BF16),
            pltpu.VMEM((4, positions, LANES), BF16),
            pltpu.VMEM((4, LANES, LANES), BF16),
            pltpu.VMEM((positions, LANES), F32),
            pltpu.VMEM((positions, LANES), F32),
            pltpu.VMEM((rows, own * LANES), BF16),
            pltpu.VMEM((own * rows, 2 * LANES), BF16),
            pltpu.VMEM((own * rows, 2 * LANES), BF16),
            pltpu.VMEM((2 * rows, own * LANES), BF16),
            pltpu.VMEM((2 * rows, own * LANES), BF16),
            pltpu.VMEM((own * rows, 2 * LANES), F32),
            pltpu.VMEM((own * rows, 2 * LANES), F32),
            pltpu.VMEM((own * rows, 2 * LANES), F32),
            pltpu.SemaphoreType.DMA((12,)),
            pltpu.SemaphoreType.DMA((11,)),
            pltpu.SemaphoreType.DMA((11,)),
            pltpu.SemaphoreType.DMA((2, 2, CHUNKS)),
            pltpu.SemaphoreType.DMA((2, 2, CHUNKS)),
            pltpu.SemaphoreType.DMA((2, CHUNKS)),
            pltpu.SemaphoreType.DMA((2, CHUNKS)),
            pltpu.SemaphoreType.DMA((3,)),
            pltpu.SemaphoreType.DMA((3,)),
        ],
        compiler_params=pltpu.CompilerParams(
            collective_id=0, has_side_effects=True, vmem_limit_bytes=40 * 1024 * 1024
        ),
        name="hyena",
    )(*map(in_hbm, (keys, values, taps, cotangent, out_weight, queries, *tables(rows), gain)))
    outs = pl.pallas_call(
        store,
        out_shape=shapes,
        in_specs=[vmem] * 7,
        out_specs=[far] * 7,
        scratch_shapes=[pltpu.SemaphoreType.DMA((7,))],
        compiler_params=pltpu.CompilerParams(vmem_limit_bytes=16 * 1024 * 1024),
        name="store",
    )(*results)
    return (*outs[:6], outs[6].reshape(LANES))


def solution(mesh):
    wide = P("seq", "chan")
    return jax.shard_map(
        functools.partial(local, mesh.shape["seq"]),
        mesh=mesh,
        in_specs=(wide, wide, wide, wide, P("chan", None), wide, P("chan")),
        out_specs=(wide, wide, wide, wide, P("chan", None), wide, P("chan")),
        check_vma=False,
    )
```

```python
import functools
import math

import jax
import jax.numpy as jnp
import numpy as np
from jax import lax
from jax.experimental import pallas as pl
from jax.experimental.pallas import tpu as pltpu
from jax.sharding import PartitionSpec as P

MESH = pl.DeviceIdType.MESH
BF16 = jnp.bfloat16
F32 = jnp.float32
LANES = 128
CHUNKS = 4
RING = 4


def split_table(table):
    high = table.astype(BF16)
    low = (table - high.astype(np.float64)).astype(BF16)
    return jnp.asarray(np.stack([high, low]))


def tables(rows):
    count = rows * LANES
    ids = np.arange(rows)
    lane = np.arange(LANES)
    first = 2.0 * np.pi * (((4 * ids[:, None] + 1) * ids[None, :]) % (4 * rows)) / (4 * rows)
    second = 2.0 * np.pi * ((lane[:, None] * lane[None, :]) % LANES) / LANES
    twist = 2.0 * np.pi * ((4 * ids[:, None] + 1) * lane[None, :]) / (4 * count)
    cos, sin = np.cos(second), np.sin(second)
    return (
        split_table(np.concatenate([np.cos(first), np.sin(first)], axis=0)),
        jnp.asarray(np.stack([np.cos(twist), np.sin(twist)]), F32),
        split_table(np.block([[cos, sin], [-sin, cos]])),
        split_table(np.block([[cos, -sin], [sin, cos]])),
        split_table(np.concatenate([np.cos(first).T, np.sin(first).T], axis=1) / count),
    )


def in_hbm(array):
    return pltpu.with_memory_space_constraint(array, pltpu.HBM)


def dot(left, right):
    return jnp.dot(left, right, preferred_element_type=F32)


def split(value):
    high = value.astype(BF16)
    return high, (value - high.astype(F32)).astype(BF16)


def kernel(
    n,
    keys_in,
    values_in,
    taps_in,
    cot_in,
    weight_in,
    queries_in,
    fa_in,
    tw_in,
    fb_in,
    gb_in,
    ga_in,
    gain_in,
    out_o,
    query_o,
    key_o,
    value_o,
    weight_o,
    taps_o,
    skip_o,
    inner_cot,
    grad_recv,
    keys,
    values,
    taps,
    cot_all,
    weight,
    queries,
    fa,
    tw,
    fb,
    gb,
    ga,
    gain,
    stage,
    first_send,
    first_recv,
    cot_send,
    cot_recv,
    conv_send,
    conv_recv,
    grad_send,
    weight_send,
    weight_recv,
    pair_send,
    pair_recv,
    total_recv,
    gated_all,
    columns,
    back,
    mixed_all,
    xb,
    t_high,
    t_low,
    d_high,
    d_low,
    spec_inner,
    spec_taps,
    spec_cot,
    table_sem,
    send_sem,
    recv_sem,
    chan_send,
    chan_recv,
    relay_send,
    relay_recv,
    col_send,
    col_recv,
):
    me = lax.axis_index("seq")
    lane = lax.axis_index("chan")
    core, chip = lax.rem(lane, 2), lane // 2
    twin = 2 * chip + 1 - core
    mirror = 2 * (1 - chip) + core
    corner = 2 * (1 - chip) + 1 - core
    positions = keys.shape[0]
    blocks = positions // LANES
    rows = n * blocks
    own = LANES // n
    piece = own * blocks
    window = positions * n
    scale = 1.0 / math.sqrt(window)

    pairs = (
        (keys_in, keys),
        (values_in, values),
        (taps_in, taps),
        (cot_in, cot_all.at[lane]),
        (weight_in, weight),
        (queries_in, queries),
        (fa_in, fa),
        (tw_in, tw),
        (fb_in, fb),
        (gb_in, gb),
        (ga_in, ga),
        (gain_in, gain),
    )
    copies = [
        pltpu.make_async_copy(src, dst, table_sem.at[i]) for i, (src, dst) in enumerate(pairs)
    ]
    plane = n // 2
    here, spot = me // plane, lax.rem(me, plane)
    across = 1 - here

    depth = plane // RING
    far_first = sorted(
        ((dz, dx) for dz in range(depth) for dx in range(RING)),
        key=lambda offset: -min(offset[0], depth - offset[0]) - min(offset[1], RING - offset[1]),
    )

    def place_at(offset):
        dz, dx = offset
        return lax.rem(spot // RING + dz, depth) * RING + lax.rem(spot + dx, RING)

    barrier = pltpu.get_barrier_semaphore()

    def greet(place):
        pl.semaphore_signal(barrier, inc=1, device_id=place, device_id_type=MESH)

    for offset in far_first:
        greet({"seq": across * plane + place_at(offset)})
    for offset in far_first[:-1]:
        greet({"seq": here * plane + place_at(offset)})
    for partner in (mirror, corner, twin):
        greet({"chan": partner})
    for copy in copies:
        copy.start()

    def send(src, dst, phase, peer):
        pltpu.make_async_remote_copy(
            src_ref=src,
            dst_ref=dst,
            send_sem=send_sem.at[phase],
            recv_sem=recv_sem.at[phase],
            device_id={"seq": peer},
            device_id_type=MESH,
        ).start()

    def exchange(src, dst, phase, half, index, part):
        def at(ref, slot):
            return ref.at[slot, index, part]

        for offset in far_first:
            if half is here and offset == (0, 0):
                continue
            peer = half * plane + place_at(offset)
            send(at(src, peer), at(dst, me), phase, peer)
        if half is here:
            dst[me, index, part] = src[me, index, part]

    def exchange_all(src, dst, phase, index=0, part=slice(None)):
        exchange(src, dst, phase, across, index, part)
        exchange(src, dst, phase, here, index, part)

    def await_all(buf, sems, phase, count=n - 1, index=None):
        part = buf.at[pl.ds(0, count)] if index is None else buf.at[pl.ds(0, count), index]
        pltpu.make_async_copy(part, part, sems.at[phase]).wait()

    def turn(value, b):
        stage[pl.ds(b, LANES, stride=blocks), :] = value.T

    def pack(value, dst, index):
        for b in range(blocks):
            turn(value(b), b)
        put(dst, index)

    def put(dst, index):
        dst[:, index] = stage[...].astype(BF16).reshape(n, piece, LANES)

    def unpack(src, index):
        stage[...] = src[:, index].astype(F32).reshape(n * piece, LANES)
        return lambda b: stage[pl.ds(b, LANES, stride=blocks), :].T

    def block(ref, b):
        return ref[b * LANES : (b + 1) * LANES, :].astype(F32)

    def gather_part(src, buf, phase, k):
        size = positions // CHUNKS
        part = pl.ds(k * size, size)
        started = [
            pltpu.make_async_remote_copy(
                src_ref=src.at[part],
                dst_ref=buf.at[lane, part],
                send_sem=chan_send.at[phase, way, k],
                recv_sem=chan_recv.at[phase, way, k],
                device_id={"chan": partner},
                device_id_type=MESH,
            )
            for way, partner in enumerate((mirror, twin))
        ]
        for copy in started:
            copy.start()
        return started

    def relay(buf, phase, started, k):
        size = positions // CHUNKS
        part = pl.ds(k * size, size)
        started[k][0].wait_recv()
        passed = pltpu.make_async_remote_copy(
            src_ref=buf.at[mirror, part],
            dst_ref=buf.at[mirror, part],
            send_sem=relay_send.at[phase, k],
            recv_sem=relay_recv.at[phase, k],
            device_id={"chan": twin},
            device_id_type=MESH,
        )
        passed.start()
        return passed

    def forward(src, index, spec, pairs):
        for pair in pairs:
            x = src[:, index, 16 * pair : 16 * pair + 16, :].astype(F32)
            for half in range(2):
                xb[:, (2 * pair + half) * LANES : (2 * pair + half + 1) * LANES] = (
                    x[:, 8 * half : 8 * half + 8, :].reshape(rows, LANES).astype(BF16)
                )
            cols = xb[:, 2 * pair * LANES : (2 * pair + 2) * LANES]
            a = dot(fa[0], cols) + dot(fa[1], cols)
            for half in range(2):
                real = a[:rows, half * LANES : (half + 1) * LANES]
                imag = a[rows:, half * LANES : (half + 1) * LANES]
                c = 2 * pair + half
                t = jnp.concatenate(
                    [real * tw[0] - imag * tw[1], real * tw[1] + imag * tw[0]], axis=1
                )
                t_high[c * rows : (c + 1) * rows, :], t_low[c * rows : (c + 1) * rows, :] = split(t)
            for c in (2 * pair, 2 * pair + 1):
                part = slice(c * rows, (c + 1) * rows)
                spec[part, :] = (
                    dot(t_high[part, :], fb[0])
                    + dot(t_high[part, :], fb[1])
                    + dot(t_low[part, :], fb[0])
                )

    def inverse(left, right, conjugate, dst, index, pairs):
        sign = -1.0 if conjugate else 1.0
        for pair in pairs:
            for c in (2 * pair, 2 * pair + 1):
                part = slice(c * rows, (c + 1) * rows)
                l_real, l_imag = left[part, :LANES], sign * left[part, LANES:]
                r_real, r_imag = right[part, :LANES], right[part, LANES:]
                high, low = split(
                    jnp.concatenate(
                        [l_real * r_real - l_imag * r_imag, l_real * r_imag + l_imag * r_real],
                        axis=1,
                    )
                )
                y = dot(high, gb[0]) + dot(high, gb[1]) + dot(low, gb[0])
                real, imag = y[:, :LANES], y[:, LANES:]
                d_real = split(real * tw[0] + imag * tw[1])
                d_imag = split(imag * tw[0] - real * tw[1])
                cols = slice(c * LANES, (c + 1) * LANES)
                d_high[:rows, cols], d_low[:rows, cols] = d_real
                d_high[rows:, cols], d_low[rows:, cols] = d_imag
            cols = slice(2 * pair * LANES, (2 * pair + 2) * LANES)
            y = dot(ga[0], d_high[:, cols]) + dot(ga[1], d_high[:, cols]) + dot(ga[0], d_low[:, cols])
            dst[:, index, 16 * pair : 16 * pair + 16, :] = jnp.concatenate(
                [y[:, :LANES].reshape(n, 8, LANES), y[:, LANES:].reshape(n, 8, LANES)], axis=1
            ).astype(BF16)

    every = range(own // 2)

    team = min(8, plane)
    first_spot, rank = spot // team * team, lax.rem(spot, team)
    height = LANES // team
    mine = pl.ds(pl.multiple_of(rank * height, height), height)
    col_copies = []
    for k, partner in enumerate((mirror, corner, twin)):
        cols = pl.ds(pl.multiple_of(partner * LANES, LANES), LANES)
        part = mine if k < 2 else pl.ds(0, LANES)
        col_copies.append(
            pltpu.make_async_remote_copy(
                src_ref=weight.at[part, cols],
                dst_ref=columns.at[lane, part],
                send_sem=col_send.at[k],
                recv_sem=col_recv.at[k],
                device_id={"chan": partner},
                device_id_type=MESH,
            )
        )
    share = 4 * LANES // plane
    count = LANES // share
    held = {}

    def inner_out():
        exchange_all(first_send, first_recv, 0, 0)

    def taps_out():
        copies[2].wait()
        pack(lambda b: block(taps, b), first_send, 1)
        exchange_all(first_send, first_recv, 8, 1)

    def signals_left():
        await_all(first_send, send_sem, 0, index=0)
        await_all(first_send, send_sem, 8, index=1)

    def cot_out():
        held["cot"] += [gather_part(cot_in, cot_all, 0, k) for k in range(1, CHUNKS)]

    def cot_start():
        held["cot"] = [gather_part(cot_in, cot_all, 0, 0)]

    def columns_out():
        copies[4].wait()
        for copy in col_copies:
            copy.start()
        columns[lane] = weight[:, pl.ds(pl.multiple_of(lane * LANES, LANES), LANES)]

    def columns_on():
        for k, origin in enumerate((mirror, corner)):
            col_copies[k].wait_recv()
            part = columns.at[origin, mine]
            for step in range(1, team):
                peer = here * plane + first_spot + lax.rem(rank + step, team)
                send(part, part, 9 + k, peer)

    def cot_signal():
        copies[3].wait()
        copies[5].wait()
        held["cot_passed"] = []
        for k in range(CHUNKS + 1):
            if k < CHUNKS:
                held["cot_passed"].append(relay(cot_all, 0, held["cot"], k))
            if k == 0:
                continue
            held["cot"][k - 1][1].wait_recv()
            held["cot_passed"][k - 1].wait_recv()
            size = blocks // CHUNKS
            for b in range((k - 1) * size, k * size):
                part = pl.ds(b * LANES, LANES)
                total = jnp.zeros((LANES, LANES), F32)
                for g in range(0, 4, 2):
                    left = jnp.concatenate([cot_all[g, part], cot_all[g + 1, part]], axis=1)
                    total += lax.dot_general(
                        left,
                        weight[:, g * LANES : (g + 2) * LANES],
                        (((1,), (1,)), ((), ())),
                        preferred_element_type=F32,
                    )
                back[part, :] = total
                signal = total * block(queries, b)
                inner_cot[part, :] = signal
                turn(signal, b)
        put(cot_send, 0)
        exchange_all(cot_send, cot_recv, 1)

    def conv_signal():
        for copy in copies[6:]:
            copy.wait()
        await_all(first_recv, recv_sem, 0, index=0)
        forward(first_recv, 0, spec_inner, every)
        await_all(first_recv, recv_sem, 8, index=1)
        forward(first_recv, 1, spec_taps, every)
        inverse(spec_taps, spec_inner, False, conv_send, 0, every)
        exchange_all(conv_send, conv_recv, 2)

    def grad_pairs(pairs):
        forward(cot_recv, 0, spec_cot, pairs)
        inverse(spec_taps, spec_cot, True, grad_send, 0, pairs)

    def grad_first():
        await_all(cot_recv, recv_sem, 1)
        grad_pairs(every)

    def grad_rest():
        exchange_all(grad_send, grad_recv, 3, 0)

    def taps_signal():
        inverse(spec_inner, spec_cot, True, grad_send, 1, every)
        exchange_all(grad_send, grad_recv, 4, 1)

    def gate():
        await_all(conv_recv, recv_sem, 2)
        conv = unpack(conv_recv, 0)
        held["gated"] = []
        for b in range(blocks):
            part = pl.ds(b * LANES, LANES)
            mixed = conv(b) + gain[...] * (block(keys, b) * block(values, b))
            mixed_all[part, :] = mixed
            gated_all[lane, part, :] = (block(queries, b) * mixed).astype(BF16)
            if (b + 1) % (blocks // CHUNKS) == 0:
                k = b // (blocks // CHUNKS)
                held["gated"].append(gather_part(gated_all.at[lane], gated_all, 1, k))
        skip = jnp.zeros((8, LANES), F32)
        for b in range(blocks):
            part = pl.ds(b * LANES, LANES)
            product = inner_cot[part, :] * (block(keys, b) * block(values, b))
            skip += jnp.sum(product.reshape(LANES // 8, 8, LANES), axis=0)
        held["skip"] = skip

    def query_grads():
        for b in range(blocks):
            part = pl.ds(b * LANES, LANES)
            query_o[part, :] = (back[part, :] * mixed_all[part, :]).astype(BF16)

    def weight_out():
        skip_high, skip_low = split(held["skip"])
        tail = jnp.concatenate([skip_high.astype(F32), skip_low.astype(F32)], axis=0).astype(BF16)
        gated = gated_all[lane].T
        for g in range(4):
            term = dot(gated, cot_all[g]).astype(BF16)
            weight_send[g * count : (g + 1) * count, :share, :] = term.reshape(count, share, LANES)
        weight_send[:, share:, :] = jnp.broadcast_to(tail[None], (plane, 16, LANES))

        for offset in far_first[:-1]:
            place = place_at(offset)
            send(weight_send.at[place], weight_recv.at[spot], 5, here * plane + place)
        weight_recv[spot] = weight_send[spot]

    def weight_pair():
        await_all(weight_recv, recv_sem, 5, plane - 1)
        sums = jnp.sum(weight_recv[...].astype(F32), axis=0)
        pair_send[:share, :] = sums[:share]
        pair_send[share:, :] = sums[share : share + 8] + sums[share + 8 :]
        send(pair_send, pair_recv, 6, across * plane + spot)

    def weight_total():
        pltpu.make_async_copy(pair_recv, pair_recv, recv_sem.at[6]).wait()
        sums = pair_send[...] + pair_recv[...]
        total_recv[spot] = sums[:share].astype(BF16)
        skip_o[...] = jnp.sum(sums[share:], axis=0, keepdims=True) * scale

        for offset in far_first[:-1]:
            send(total_recv.at[spot], total_recv.at[spot], 7, here * plane + place_at(offset))

    def gated_relay():
        held["gated_passed"] = [relay(gated_all, 1, held["gated"], k) for k in range(CHUNKS)]

    def project():
        for copy in [pair[1] for pair in held["gated"]] + held["gated_passed"] + col_copies[2:]:
            copy.wait_recv()
        others = columns.at[0, pl.ds(0, LANES - height)]
        for phase in (9, 10):
            pltpu.make_async_copy(others, others, recv_sem.at[phase]).wait()
        half = positions // 2
        for k in range(2):
            part = pl.ds(k * half, half)
            total = jnp.zeros((half, LANES), F32)
            for g in range(0, 4, 2):
                left = jnp.concatenate([gated_all[g, part], gated_all[g + 1, part]], axis=1)
                total += dot(left, columns[g : g + 2].reshape(2 * LANES, LANES))
            out_o[part, :] = total.astype(BF16)

    def factor_grads():
        await_all(grad_recv, recv_sem, 3, index=0)
        grad = unpack(grad_recv, 0)
        for b in range(blocks):
            part = pl.ds(b * LANES, LANES)
            inner_grad = grad(b) + gain[...] * inner_cot[part, :]
            key_o[part, :] = (inner_grad * block(values, b)).astype(BF16)
            value_o[part, :] = (inner_grad * block(keys, b)).astype(BF16)

    def taps_grads():
        await_all(grad_recv, recv_sem, 4, index=1)
        grad = unpack(grad_recv, 1)
        for b in range(blocks):
            taps_o[pl.ds(b * LANES, LANES), :] = grad(b) * scale

    def settle():
        await_all(total_recv, recv_sem, 7, plane - 1)
        for g in range(4):
            weight_o[:, g * LANES : (g + 1) * LANES] = (
                total_recv[g * count : (g + 1) * count].astype(F32).reshape(LANES, LANES) * scale
            )
        await_all(cot_send, send_sem, 1)
        await_all(conv_send, send_sem, 2)
        await_all(grad_send, send_sem, 3, index=0)
        await_all(grad_send, send_sem, 4, index=1)
        await_all(weight_send, send_sem, 5, plane - 1)
        pltpu.make_async_copy(pair_send, pair_send, send_sem.at[6]).wait()
        await_all(total_recv, send_sem, 7, plane - 1)
        for name in ("cot", "gated"):
            for copy in sum(held[name], held[name + "_passed"]):
                copy.wait_send()
        others = columns.at[0, pl.ds(0, LANES - height)]
        for phase in (9, 10):
            pltpu.make_async_copy(others, others, send_sem.at[phase]).wait()
        for copy in col_copies:
            copy.wait_send()

    copies[0].wait()
    copies[1].wait()
    pack(lambda b: block(keys, b) * block(values, b), first_send, 0)
    pl.semaphore_wait(barrier, n + 2)
    for step in (
        cot_start,
        inner_out,
        taps_out,
        cot_out,
        conv_signal,
        columns_out,
        cot_signal,
        gate,
        weight_out,
        columns_on,
        grad_first,
        weight_pair,
        grad_rest,
        taps_signal,
        query_grads,
        weight_total,
        gated_relay,
        signals_left,
        project,
        factor_grads,
        taps_grads,
        settle,
    ):
        step()


def store(*refs):
    count = len(refs) // 2
    copies = [
        pltpu.make_async_copy(refs[i], refs[count + i], refs[-1].at[i]) for i in range(count)
    ]
    for copy in copies:
        copy.start()
    for copy in copies:
        copy.wait()


def local(n, queries, keys, values, cotangent, out_weight, taps, skip_gain):
    positions = keys.shape[0]
    blocks = positions // LANES
    rows = n * blocks
    own = LANES // n
    piece = own * blocks
    plane = n // 2
    share = 4 * LANES // plane
    vmem = pl.BlockSpec(memory_space=pltpu.VMEM)
    far = pl.BlockSpec(memory_space=pltpu.HBM)
    wide = jax.ShapeDtypeStruct((positions, LANES), BF16)
    wide_f32 = jax.ShapeDtypeStruct((positions, LANES), F32)
    square = jax.ShapeDtypeStruct((LANES, 4 * LANES), F32)
    line = jax.ShapeDtypeStruct((1, LANES), F32)
    gain = skip_gain.reshape(1, LANES)

    def buffer(count):
        return pltpu.VMEM((n, count, piece, LANES), BF16)

    shapes = [wide, wide, wide, wide, square, wide_f32, line]
    results = pl.pallas_call(
        functools.partial(kernel, n),
        out_shape=shapes,
        in_specs=[far] * 12,
        out_specs=[vmem] * 7,
        scratch_shapes=[
            pltpu.VMEM((positions, LANES), F32),
            buffer(2),
            pltpu.VMEM((positions, LANES), BF16),
            pltpu.VMEM((positions, LANES), BF16),
            pltpu.VMEM((positions, LANES), F32),
            pltpu.VMEM((4, positions, LANES), BF16),
            pltpu.VMEM((LANES, 4 * LANES), BF16),
            pltpu.VMEM((positions, LANES), BF16),
            pltpu.VMEM((2, 2 * rows, rows), BF16),
            pltpu.VMEM((2, rows, LANES), F32),
            pltpu.VMEM((2, 2 * LANES, 2 * LANES), BF16),
            pltpu.VMEM((2, 2 * LANES, 2 * LANES), BF16),
            pltpu.VMEM((2, rows, 2 * rows), BF16),
            pltpu.VMEM((1, LANES), F32),
            pltpu.VMEM((positions, LANES), F32),
            buffer(2),
            buffer(2),
            buffer(1),
            buffer(1),
            buffer(1),
            buffer(1),
            buffer(2),
            pltpu.VMEM((plane, share + 16, LANES), BF16),
            pltpu.VMEM((plane, share + 16, LANES), BF16),
            pltpu.VMEM((share + 8, LANES), F32),
            pltpu.VMEM((share + 8, LANES), F32),
            pltpu.VMEM((plane, share, LANES), BF16),
            pltpu.VMEM((4, positions, LANES), BF16),
            pltpu.VMEM((4, LANES, LANES), BF16),
            pltpu.VMEM((positions, LANES), F32),
            pltpu.VMEM((positions, LANES), F32),
            pltpu.VMEM((rows, own * LANES), BF16),
            pltpu.VMEM((own * rows, 2 * LANES), BF16),
            pltpu.VMEM((own * rows, 2 * LANES), BF16),
            pltpu.VMEM((2 * rows, own * LANES), BF16),
            pltpu.VMEM((2 * rows, own * LANES), BF16),
            pltpu.VMEM((own * rows, 2 * LANES), F32),
            pltpu.VMEM((own * rows, 2 * LANES), F32),
            pltpu.VMEM((own * rows, 2 * LANES), F32),
            pltpu.SemaphoreType.DMA((12,)),
            pltpu.SemaphoreType.DMA((11,)),
            pltpu.SemaphoreType.DMA((11,)),
            pltpu.SemaphoreType.DMA((2, 2, CHUNKS)),
            pltpu.SemaphoreType.DMA((2, 2, CHUNKS)),
            pltpu.SemaphoreType.DMA((2, CHUNKS)),
            pltpu.SemaphoreType.DMA((2, CHUNKS)),
            pltpu.SemaphoreType.DMA((3,)),
            pltpu.SemaphoreType.DMA((3,)),
        ],
        compiler_params=pltpu.CompilerParams(
            collective_id=0, has_side_effects=True, vmem_limit_bytes=40 * 1024 * 1024
        ),
        name="hyena",
    )(*map(in_hbm, (keys, values, taps, cotangent, out_weight, queries, *tables(rows), gain)))
    outs = pl.pallas_call(
        store,
        out_shape=shapes,
        in_specs=[vmem] * 7,
        out_specs=[far] * 7,
        scratch_shapes=[pltpu.SemaphoreType.DMA((7,))],
        compiler_params=pltpu.CompilerParams(vmem_limit_bytes=16 * 1024 * 1024),
        name="store",
    )(*results)
    return (*outs[:6], outs[6].reshape(LANES))


def solution(mesh):
    wide = P("seq", "chan")
    return jax.shard_map(
        functools.partial(local, mesh.shape["seq"]),
        mesh=mesh,
        in_specs=(wide, wide, wide, wide, P("chan", None), wide, P("chan")),
        out_specs=(wide, wide, wide, wide, P("chan", None), wide, P("chan")),
        check_vma=False,
    )
```

```python
import functools
import math

import jax
import jax.numpy as jnp
import numpy as np
from jax import lax
from jax.experimental import pallas as pl
from jax.experimental.pallas import tpu as pltpu
from jax.sharding import PartitionSpec as P

MESH = pl.DeviceIdType.MESH
BF16 = jnp.bfloat16
F32 = jnp.float32
LANES = 128
CHUNKS = 4
RING = 4


def split_table(table):
    high = table.astype(BF16)
    low = (table - high.astype(np.float64)).astype(BF16)
    return jnp.asarray(np.stack([high, low]))


def tables(rows):
    count = rows * LANES
    ids = np.arange(rows)
    lane = np.arange(LANES)
    first = 2.0 * np.pi * (((4 * ids[:, None] + 1) * ids[None, :]) % (4 * rows)) / (4 * rows)
    second = 2.0 * np.pi * ((lane[:, None] * lane[None, :]) % LANES) / LANES
    twist = 2.0 * np.pi * ((4 * ids[:, None] + 1) * lane[None, :]) / (4 * count)
    cos, sin = np.cos(second), np.sin(second)
    return (
        split_table(np.concatenate([np.cos(first), np.sin(first)], axis=0)),
        jnp.asarray(np.stack([np.cos(twist), np.sin(twist)]), F32),
        split_table(np.block([[cos, sin], [-sin, cos]])),
        split_table(np.block([[cos, -sin], [sin, cos]])),
        split_table(np.concatenate([np.cos(first).T, np.sin(first).T], axis=1) / count),
    )


def in_hbm(array):
    return pltpu.with_memory_space_constraint(array, pltpu.HBM)


def dot(left, right):
    return jnp.dot(left, right, preferred_element_type=F32)


def split(value):
    high = value.astype(BF16)
    return high, (value - high.astype(F32)).astype(BF16)


def kernel(
    n,
    keys_in,
    values_in,
    taps_in,
    cot_in,
    weight_in,
    queries_in,
    fa_in,
    tw_in,
    fb_in,
    gb_in,
    ga_in,
    gain_in,
    out_o,
    query_o,
    key_o,
    value_o,
    weight_o,
    grad_recv,
    skip_o,
    inner_cot,
    keys,
    values,
    taps,
    cot_all,
    weight,
    queries,
    fa,
    tw,
    fb,
    gb,
    ga,
    gain,
    stage,
    first_send,
    first_recv,
    cot_send,
    cot_recv,
    conv_send,
    conv_recv,
    grad_send,
    weight_send,
    weight_recv,
    pair_send,
    pair_recv,
    total_recv,
    gated_all,
    columns,
    back,
    mixed_all,
    xb,
    t_high,
    t_low,
    d_high,
    d_low,
    spec_inner,
    spec_taps,
    spec_cot,
    table_sem,
    send_sem,
    recv_sem,
    chan_send,
    chan_recv,
    relay_send,
    relay_recv,
    col_send,
    col_recv,
):
    me = lax.axis_index("seq")
    lane = lax.axis_index("chan")
    core, chip = lax.rem(lane, 2), lane // 2
    twin = 2 * chip + 1 - core
    mirror = 2 * (1 - chip) + core
    corner = 2 * (1 - chip) + 1 - core
    positions = keys.shape[0]
    blocks = positions // LANES
    rows = n * blocks
    own = LANES // n
    piece = own * blocks
    window = positions * n
    scale = 1.0 / math.sqrt(window)

    pairs = (
        (keys_in, keys),
        (values_in, values),
        (taps_in, taps),
        (cot_in, cot_all.at[lane]),
        (weight_in, weight),
        (queries_in, queries),
        (fa_in, fa),
        (tw_in, tw),
        (fb_in, fb),
        (gb_in, gb),
        (ga_in, ga),
        (gain_in, gain),
    )
    copies = [
        pltpu.make_async_copy(src, dst, table_sem.at[i]) for i, (src, dst) in enumerate(pairs)
    ]
    plane = n // 2
    here, spot = me // plane, lax.rem(me, plane)
    across = 1 - here

    depth = plane // RING
    far_first = sorted(
        ((dz, dx) for dz in range(depth) for dx in range(RING)),
        key=lambda offset: -min(offset[0], depth - offset[0]) - min(offset[1], RING - offset[1]),
    )

    def place_at(offset):
        dz, dx = offset
        return lax.rem(spot // RING + dz, depth) * RING + lax.rem(spot + dx, RING)

    barrier = pltpu.get_barrier_semaphore()

    def greet(place):
        pl.semaphore_signal(barrier, inc=1, device_id=place, device_id_type=MESH)

    for offset in far_first:
        greet({"seq": across * plane + place_at(offset)})
    for offset in far_first[:-1]:
        greet({"seq": here * plane + place_at(offset)})
    for partner in (mirror, corner, twin):
        greet({"chan": partner})
    for copy in copies:
        copy.start()

    def send(src, dst, phase, peer):
        pltpu.make_async_remote_copy(
            src_ref=src,
            dst_ref=dst,
            send_sem=send_sem.at[phase],
            recv_sem=recv_sem.at[phase],
            device_id={"seq": peer},
            device_id_type=MESH,
        ).start()

    def exchange(src, dst, phase, half, index, part):
        def at(ref, slot):
            return ref.at[slot, index, part]

        for offset in far_first:
            if half is here and offset == (0, 0):
                continue
            peer = half * plane + place_at(offset)
            send(at(src, peer), at(dst, me), phase, peer)
        if half is here:
            dst[me, index, part] = src[me, index, part]

    def exchange_all(src, dst, phase, index=0, part=slice(None)):
        exchange(src, dst, phase, across, index, part)
        exchange(src, dst, phase, here, index, part)

    def await_all(buf, sems, phase, count=n - 1, index=None):
        part = buf.at[pl.ds(0, count)] if index is None else buf.at[pl.ds(0, count), index]
        pltpu.make_async_copy(part, part, sems.at[phase]).wait()

    def turn(value, b):
        stage[pl.ds(b, LANES, stride=blocks), :] = value.T

    def pack(value, dst, index):
        for b in range(blocks):
            turn(value(b), b)
        put(dst, index)

    def put(dst, index):
        dst[:, index] = stage[...].astype(BF16).reshape(n, piece, LANES)

    def unpack(src, index):
        stage[...] = src[:, index].astype(F32).reshape(n * piece, LANES)
        return lambda b: stage[pl.ds(b, LANES, stride=blocks), :].T

    def block(ref, b):
        return ref[b * LANES : (b + 1) * LANES, :].astype(F32)

    def gather_part(src, buf, phase, k):
        size = positions // CHUNKS
        part = pl.ds(k * size, size)
        started = [
            pltpu.make_async_remote_copy(
                src_ref=src.at[part],
                dst_ref=buf.at[lane, part],
                send_sem=chan_send.at[phase, way, k],
                recv_sem=chan_recv.at[phase, way, k],
                device_id={"chan": partner},
                device_id_type=MESH,
            )
            for way, partner in enumerate((mirror, twin))
        ]
        for copy in started:
            copy.start()
        return started

    def relay(buf, phase, started, k):
        size = positions // CHUNKS
        part = pl.ds(k * size, size)
        started[k][0].wait_recv()
        passed = pltpu.make_async_remote_copy(
            src_ref=buf.at[mirror, part],
            dst_ref=buf.at[mirror, part],
            send_sem=relay_send.at[phase, k],
            recv_sem=relay_recv.at[phase, k],
            device_id={"chan": twin},
            device_id_type=MESH,
        )
        passed.start()
        return passed

    def forward(src, index, spec, pairs):
        for pair in pairs:
            x = src[:, index, 16 * pair : 16 * pair + 16, :].astype(F32)
            for half in range(2):
                xb[:, (2 * pair + half) * LANES : (2 * pair + half + 1) * LANES] = (
                    x[:, 8 * half : 8 * half + 8, :].reshape(rows, LANES).astype(BF16)
                )
            cols = xb[:, 2 * pair * LANES : (2 * pair + 2) * LANES]
            a = dot(fa[0], cols) + dot(fa[1], cols)
            for half in range(2):
                real = a[:rows, half * LANES : (half + 1) * LANES]
                imag = a[rows:, half * LANES : (half + 1) * LANES]
                c = 2 * pair + half
                t = jnp.concatenate(
                    [real * tw[0] - imag * tw[1], real * tw[1] + imag * tw[0]], axis=1
                )
                t_high[c * rows : (c + 1) * rows, :], t_low[c * rows : (c + 1) * rows, :] = split(t)
            for c in (2 * pair, 2 * pair + 1):
                part = slice(c * rows, (c + 1) * rows)
                spec[part, :] = (
                    dot(t_high[part, :], fb[0])
                    + dot(t_high[part, :], fb[1])
                    + dot(t_low[part, :], fb[0])
                )

    def inverse(left, right, conjugate, dst, index, pairs):
        sign = -1.0 if conjugate else 1.0
        for pair in pairs:
            for c in (2 * pair, 2 * pair + 1):
                part = slice(c * rows, (c + 1) * rows)
                l_real, l_imag = left[part, :LANES], sign * left[part, LANES:]
                r_real, r_imag = right[part, :LANES], right[part, LANES:]
                high, low = split(
                    jnp.concatenate(
                        [l_real * r_real - l_imag * r_imag, l_real * r_imag + l_imag * r_real],
                        axis=1,
                    )
                )
                y = dot(high, gb[0]) + dot(high, gb[1]) + dot(low, gb[0])
                real, imag = y[:, :LANES], y[:, LANES:]
                d_real = split(real * tw[0] + imag * tw[1])
                d_imag = split(imag * tw[0] - real * tw[1])
                cols = slice(c * LANES, (c + 1) * LANES)
                d_high[:rows, cols], d_low[:rows, cols] = d_real
                d_high[rows:, cols], d_low[rows:, cols] = d_imag
            cols = slice(2 * pair * LANES, (2 * pair + 2) * LANES)
            y = dot(ga[0], d_high[:, cols]) + dot(ga[1], d_high[:, cols]) + dot(ga[0], d_low[:, cols])
            dst[:, index, 16 * pair : 16 * pair + 16, :] = jnp.concatenate(
                [y[:, :LANES].reshape(n, 8, LANES), y[:, LANES:].reshape(n, 8, LANES)], axis=1
            ).astype(BF16)

    every = range(own // 2)

    team = min(8, plane)
    first_spot, rank = spot // team * team, lax.rem(spot, team)
    height = LANES // team
    mine = pl.ds(pl.multiple_of(rank * height, height), height)
    col_copies = []
    for k, partner in enumerate((mirror, corner, twin)):
        cols = pl.ds(pl.multiple_of(partner * LANES, LANES), LANES)
        part = mine if k < 2 else pl.ds(0, LANES)
        col_copies.append(
            pltpu.make_async_remote_copy(
                src_ref=weight.at[part, cols],
                dst_ref=columns.at[lane, part],
                send_sem=col_send.at[k],
                recv_sem=col_recv.at[k],
                device_id={"chan": partner},
                device_id_type=MESH,
            )
        )
    share = 4 * LANES // plane
    count = LANES // share
    held = {}

    def inner_out():
        exchange_all(first_send, first_recv, 0, 0)

    def taps_out():
        copies[2].wait()
        pack(lambda b: block(taps, b), first_send, 1)
        exchange_all(first_send, first_recv, 8, 1)

    def signals_left():
        await_all(first_send, send_sem, 0, index=0)
        await_all(first_send, send_sem, 8, index=1)

    def cot_out():
        held["cot"] += [gather_part(cot_in, cot_all, 0, k) for k in range(1, CHUNKS)]

    def cot_start():
        held["cot"] = [gather_part(cot_in, cot_all, 0, 0)]

    def columns_out():
        copies[4].wait()
        for copy in col_copies:
            copy.start()
        columns[lane] = weight[:, pl.ds(pl.multiple_of(lane * LANES, LANES), LANES)]

    def columns_on():
        for k, origin in enumerate((mirror, corner)):
            col_copies[k].wait_recv()
            part = columns.at[origin, mine]
            for step in range(1, team):
                peer = here * plane + first_spot + lax.rem(rank + step, team)
                send(part, part, 9 + k, peer)

    def cot_signal():
        copies[3].wait()
        copies[5].wait()
        held["cot_passed"] = []
        for k in range(CHUNKS + 1):
            if k < CHUNKS:
                held["cot_passed"].append(relay(cot_all, 0, held["cot"], k))
            if k == 0:
                continue
            held["cot"][k - 1][1].wait_recv()
            held["cot_passed"][k - 1].wait_recv()
            size = blocks // CHUNKS
            for b in range((k - 1) * size, k * size):
                part = pl.ds(b * LANES, LANES)
                total = jnp.zeros((LANES, LANES), F32)
                for g in range(0, 4, 2):
                    left = jnp.concatenate([cot_all[g, part], cot_all[g + 1, part]], axis=1)
                    total += lax.dot_general(
                        left,
                        weight[:, g * LANES : (g + 2) * LANES],
                        (((1,), (1,)), ((), ())),
                        preferred_element_type=F32,
                    )
                back[part, :] = total
                signal = total * block(queries, b)
                inner_cot[part, :] = signal
                turn(signal, b)
        put(cot_send, 0)
        exchange_all(cot_send, cot_recv, 1)

    def conv_signal():
        for copy in copies[6:]:
            copy.wait()
        await_all(first_recv, recv_sem, 0, index=0)
        forward(first_recv, 0, spec_inner, every)
        await_all(first_recv, recv_sem, 8, index=1)
        forward(first_recv, 1, spec_taps, every)
        inverse(spec_taps, spec_inner, False, conv_send, 0, every)
        exchange_all(conv_send, conv_recv, 2)

    def grad_signal():
        await_all(cot_recv, recv_sem, 1)
        forward(cot_recv, 0, spec_cot, every)
        inverse(spec_taps, spec_cot, True, grad_send, 0, every)

    def grad_out():
        exchange_all(grad_send, grad_recv, 3, 0)

    def taps_signal():
        inverse(spec_inner, spec_cot, True, grad_send, 1, every)

    def taps_grad_out():
        exchange_all(grad_send, grad_recv, 4, 1)

    def gate():
        await_all(conv_recv, recv_sem, 2)
        conv = unpack(conv_recv, 0)
        held["gated"] = []
        for b in range(blocks):
            part = pl.ds(b * LANES, LANES)
            mixed = conv(b) + gain[...] * (block(keys, b) * block(values, b))
            mixed_all[part, :] = mixed
            gated_all[lane, part, :] = (block(queries, b) * mixed).astype(BF16)
            if (b + 1) % (blocks // CHUNKS) == 0:
                k = b // (blocks // CHUNKS)
                held["gated"].append(gather_part(gated_all.at[lane], gated_all, 1, k))

    def skip_sum():
        skip = jnp.zeros((8, LANES), F32)
        for b in range(blocks):
            part = pl.ds(b * LANES, LANES)
            product = inner_cot[part, :] * (block(keys, b) * block(values, b))
            skip += jnp.sum(product.reshape(LANES // 8, 8, LANES), axis=0)
        held["skip"] = skip

    def query_grads():
        for b in range(blocks):
            part = pl.ds(b * LANES, LANES)
            query_o[part, :] = (back[part, :] * mixed_all[part, :]).astype(BF16)

    def weight_out():
        skip_high, skip_low = split(held["skip"])
        tail = jnp.concatenate([skip_high.astype(F32), skip_low.astype(F32)], axis=0).astype(BF16)
        gated = gated_all[lane].T
        for g in range(4):
            term = dot(gated, cot_all[g]).astype(BF16)
            weight_send[g * count : (g + 1) * count, :share, :] = term.reshape(count, share, LANES)
        weight_send[:, share:, :] = jnp.broadcast_to(tail[None], (plane, 16, LANES))

        for offset in far_first[:-1]:
            place = place_at(offset)
            send(weight_send.at[place], weight_recv.at[spot], 5, here * plane + place)
        weight_recv[spot] = weight_send[spot]

    def weight_pair():
        await_all(weight_recv, recv_sem, 5, plane - 1)
        sums = jnp.sum(weight_recv[...].astype(F32), axis=0)
        pair_send[:share, :] = sums[:share]
        pair_send[share:, :] = sums[share : share + 8] + sums[share + 8 :]
        send(pair_send, pair_recv, 6, across * plane + spot)

    def weight_total():
        pltpu.make_async_copy(pair_recv, pair_recv, recv_sem.at[6]).wait()
        sums = pair_send[...] + pair_recv[...]
        total_recv[spot] = sums[:share].astype(BF16)
        skip_o[...] = jnp.sum(sums[share:], axis=0, keepdims=True) * scale

        for offset in far_first[:-1]:
            send(total_recv.at[spot], total_recv.at[spot], 7, here * plane + place_at(offset))

    def gated_relay():
        held["gated_passed"] = [relay(gated_all, 1, held["gated"], k) for k in range(CHUNKS)]

    def project():
        for copy in [pair[1] for pair in held["gated"]] + held["gated_passed"] + col_copies[2:]:
            copy.wait_recv()
        others = columns.at[0, pl.ds(0, LANES - height)]
        for phase in (9, 10):
            pltpu.make_async_copy(others, others, recv_sem.at[phase]).wait()
        half = positions // 2
        for k in range(2):
            part = pl.ds(k * half, half)
            total = jnp.zeros((half, LANES), F32)
            for g in range(0, 4, 2):
                left = jnp.concatenate([gated_all[g, part], gated_all[g + 1, part]], axis=1)
                total += dot(left, columns[g : g + 2].reshape(2 * LANES, LANES))
            out_o[part, :] = total.astype(BF16)

    def factor_grads():
        await_all(grad_recv, recv_sem, 3, index=0)
        grad = unpack(grad_recv, 0)
        for b in range(blocks):
            part = pl.ds(b * LANES, LANES)
            inner_grad = grad(b) + gain[...] * inner_cot[part, :]
            key_o[part, :] = (inner_grad * block(values, b)).astype(BF16)
            value_o[part, :] = (inner_grad * block(keys, b)).astype(BF16)

    def settle():
        await_all(grad_recv, recv_sem, 4, index=1)
        await_all(total_recv, recv_sem, 7, plane - 1)
        for g in range(4):
            weight_o[:, g * LANES : (g + 1) * LANES] = (
                total_recv[g * count : (g + 1) * count].astype(F32).reshape(LANES, LANES) * scale
            )
        await_all(cot_send, send_sem, 1)
        await_all(conv_send, send_sem, 2)
        await_all(grad_send, send_sem, 3, index=0)
        await_all(grad_send, send_sem, 4, index=1)
        await_all(weight_send, send_sem, 5, plane - 1)
        pltpu.make_async_copy(pair_send, pair_send, send_sem.at[6]).wait()
        await_all(total_recv, send_sem, 7, plane - 1)
        for name in ("cot", "gated"):
            for copy in sum(held[name], held[name + "_passed"]):
                copy.wait_send()
        others = columns.at[0, pl.ds(0, LANES - height)]
        for phase in (9, 10):
            pltpu.make_async_copy(others, others, send_sem.at[phase]).wait()
        for copy in col_copies:
            copy.wait_send()

    copies[0].wait()
    copies[1].wait()
    pack(lambda b: block(keys, b) * block(values, b), first_send, 0)
    pl.semaphore_wait(barrier, n + 2)
    for step in (
        cot_start,
        inner_out,
        taps_out,
        cot_out,
        conv_signal,
        columns_out,
        cot_signal,
        skip_sum,
        gate,
        weight_out,
        columns_on,
        grad_signal,
        weight_pair,
        grad_out,
        taps_signal,
        weight_total,
        taps_grad_out,
        query_grads,
        gated_relay,
        signals_left,
        project,
        factor_grads,
        settle,
    ):
        step()


def store(scale, *refs):
    sources, places, (stage, taps, sems) = list(refs[:7]), refs[7:14], refs[14:]
    grad, sources[5] = sources[5], taps
    copies = [
        pltpu.make_async_copy(src, dst, sems.at[i])
        for i, (src, dst) in enumerate(zip(sources, places))
    ]
    for copy in copies[:5] + copies[6:]:
        copy.start()
    positions = taps.shape[0]
    blocks = positions // LANES
    stage[...] = grad[:, 1].astype(F32).reshape(positions, LANES)
    for b in range(blocks):
        taps[pl.ds(b * LANES, LANES), :] = stage[pl.ds(b, LANES, stride=blocks), :].T * scale
    copies[5].start()
    for copy in copies:
        copy.wait()


def local(n, queries, keys, values, cotangent, out_weight, taps, skip_gain):
    positions = keys.shape[0]
    blocks = positions // LANES
    rows = n * blocks
    own = LANES // n
    piece = own * blocks
    plane = n // 2
    share = 4 * LANES // plane
    vmem = pl.BlockSpec(memory_space=pltpu.VMEM)
    far = pl.BlockSpec(memory_space=pltpu.HBM)
    wide = jax.ShapeDtypeStruct((positions, LANES), BF16)
    wide_f32 = jax.ShapeDtypeStruct((positions, LANES), F32)
    square = jax.ShapeDtypeStruct((LANES, 4 * LANES), F32)
    line = jax.ShapeDtypeStruct((1, LANES), F32)
    gain = skip_gain.reshape(1, LANES)

    def buffer(count):
        return pltpu.VMEM((n, count, piece, LANES), BF16)

    shapes = [wide, wide, wide, wide, square, wide_f32, line]
    results = pl.pallas_call(
        functools.partial(kernel, n),
        out_shape=[*shapes[:5], jax.ShapeDtypeStruct((n, 2, piece, LANES), BF16), line],
        in_specs=[far] * 12,
        out_specs=[vmem] * 7,
        scratch_shapes=[
            pltpu.VMEM((positions, LANES), F32),
            pltpu.VMEM((positions, LANES), BF16),
            pltpu.VMEM((positions, LANES), BF16),
            pltpu.VMEM((positions, LANES), F32),
            pltpu.VMEM((4, positions, LANES), BF16),
            pltpu.VMEM((LANES, 4 * LANES), BF16),
            pltpu.VMEM((positions, LANES), BF16),
            pltpu.VMEM((2, 2 * rows, rows), BF16),
            pltpu.VMEM((2, rows, LANES), F32),
            pltpu.VMEM((2, 2 * LANES, 2 * LANES), BF16),
            pltpu.VMEM((2, 2 * LANES, 2 * LANES), BF16),
            pltpu.VMEM((2, rows, 2 * rows), BF16),
            pltpu.VMEM((1, LANES), F32),
            pltpu.VMEM((positions, LANES), F32),
            buffer(2),
            buffer(2),
            buffer(1),
            buffer(1),
            buffer(1),
            buffer(1),
            buffer(2),
            pltpu.VMEM((plane, share + 16, LANES), BF16),
            pltpu.VMEM((plane, share + 16, LANES), BF16),
            pltpu.VMEM((share + 8, LANES), F32),
            pltpu.VMEM((share + 8, LANES), F32),
            pltpu.VMEM((plane, share, LANES), BF16),
            pltpu.VMEM((4, positions, LANES), BF16),
            pltpu.VMEM((4, LANES, LANES), BF16),
            pltpu.VMEM((positions, LANES), F32),
            pltpu.VMEM((positions, LANES), F32),
            pltpu.VMEM((rows, own * LANES), BF16),
            pltpu.VMEM((own * rows, 2 * LANES), BF16),
            pltpu.VMEM((own * rows, 2 * LANES), BF16),
            pltpu.VMEM((2 * rows, own * LANES), BF16),
            pltpu.VMEM((2 * rows, own * LANES), BF16),
            pltpu.VMEM((own * rows, 2 * LANES), F32),
            pltpu.VMEM((own * rows, 2 * LANES), F32),
            pltpu.VMEM((own * rows, 2 * LANES), F32),
            pltpu.SemaphoreType.DMA((12,)),
            pltpu.SemaphoreType.DMA((11,)),
            pltpu.SemaphoreType.DMA((11,)),
            pltpu.SemaphoreType.DMA((2, 2, CHUNKS)),
            pltpu.SemaphoreType.DMA((2, 2, CHUNKS)),
            pltpu.SemaphoreType.DMA((2, CHUNKS)),
            pltpu.SemaphoreType.DMA((2, CHUNKS)),
            pltpu.SemaphoreType.DMA((3,)),
            pltpu.SemaphoreType.DMA((3,)),
        ],
        compiler_params=pltpu.CompilerParams(
            collective_id=0, has_side_effects=True, vmem_limit_bytes=40 * 1024 * 1024
        ),
        name="hyena",
    )(*map(in_hbm, (keys, values, taps, cotangent, out_weight, queries, *tables(rows), gain)))
    outs = pl.pallas_call(
        functools.partial(store, 1.0 / math.sqrt(positions * n)),
        out_shape=shapes,
        in_specs=[vmem] * 7,
        out_specs=[far] * 7,
        scratch_shapes=[
            pltpu.VMEM((positions, LANES), F32),
            pltpu.VMEM((positions, LANES), F32),
            pltpu.SemaphoreType.DMA((7,)),
        ],
        compiler_params=pltpu.CompilerParams(vmem_limit_bytes=16 * 1024 * 1024),
        name="store",
    )(*results)
    return (*outs[:6], outs[6].reshape(LANES))


def solution(mesh):
    wide = P("seq", "chan")
    return jax.shard_map(
        functools.partial(local, mesh.shape["seq"]),
        mesh=mesh,
        in_specs=(wide, wide, wide, wide, P("chan", None), wide, P("chan")),
        out_specs=(wide, wide, wide, wide, P("chan", None), wide, P("chan")),
        check_vma=False,
    )
```

```python
import functools
import math

import jax
import jax.numpy as jnp
import numpy as np
from jax import lax
from jax.experimental import pallas as pl
from jax.experimental.pallas import tpu as pltpu
from jax.sharding import PartitionSpec as P

MESH = pl.DeviceIdType.MESH
BF16 = jnp.bfloat16
F32 = jnp.float32
LANES = 128
CHUNKS = 4
RING = 4


def split_table(table):
    high = table.astype(BF16)
    low = (table - high.astype(np.float64)).astype(BF16)
    return jnp.asarray(np.stack([high, low]))


def tables(rows):
    count = rows * LANES
    ids = np.arange(rows)
    lane = np.arange(LANES)
    first = 2.0 * np.pi * (((4 * ids[:, None] + 1) * ids[None, :]) % (4 * rows)) / (4 * rows)
    second = 2.0 * np.pi * ((lane[:, None] * lane[None, :]) % LANES) / LANES
    twist = 2.0 * np.pi * ((4 * ids[:, None] + 1) * lane[None, :]) / (4 * count)
    cos, sin = np.cos(second), np.sin(second)
    return (
        split_table(np.concatenate([np.cos(first), np.sin(first)], axis=0)),
        jnp.asarray(np.stack([np.cos(twist), np.sin(twist)]), F32),
        split_table(np.block([[cos, sin], [-sin, cos]])),
        split_table(np.block([[cos, -sin], [sin, cos]])),
        split_table(np.concatenate([np.cos(first).T, np.sin(first).T], axis=1) / count),
    )


def in_hbm(array):
    return pltpu.with_memory_space_constraint(array, pltpu.HBM)


def dot(left, right):
    return jnp.dot(left, right, preferred_element_type=F32)


def split(value):
    high = value.astype(BF16)
    return high, (value - high.astype(F32)).astype(BF16)


def kernel(
    n,
    keys_in,
    values_in,
    taps_in,
    cot_in,
    weight_in,
    queries_in,
    fa_in,
    tw_in,
    fb_in,
    gb_in,
    ga_in,
    gain_in,
    out_o,
    query_o,
    key_o,
    value_o,
    total_recv,
    grad_recv,
    skip_o,
    inner_cot,
    keys,
    values,
    taps,
    cot_all,
    weight,
    queries,
    fa,
    tw,
    fb,
    gb,
    ga,
    gain,
    stage,
    first_send,
    first_recv,
    cot_send,
    cot_recv,
    conv_send,
    conv_recv,
    grad_send,
    skip_recv,
    weight_send,
    weight_recv,
    pair_send,
    pair_recv,
    gated_all,
    columns,
    back,
    mixed_all,
    xb,
    t_high,
    t_low,
    d_high,
    d_low,
    spec_inner,
    spec_taps,
    spec_cot,
    table_sem,
    send_sem,
    recv_sem,
    chan_send,
    chan_recv,
    relay_send,
    relay_recv,
    col_send,
    col_recv,
):
    me = lax.axis_index("seq")
    lane = lax.axis_index("chan")
    core, chip = lax.rem(lane, 2), lane // 2
    twin = 2 * chip + 1 - core
    mirror = 2 * (1 - chip) + core
    corner = 2 * (1 - chip) + 1 - core
    positions = keys.shape[0]
    blocks = positions // LANES
    rows = n * blocks
    own = LANES // n
    piece = own * blocks
    window = positions * n
    scale = 1.0 / math.sqrt(window)

    pairs = (
        (keys_in, keys),
        (values_in, values),
        (taps_in, taps),
        (cot_in, cot_all.at[lane]),
        (weight_in, weight),
        (queries_in, queries),
        (fa_in, fa),
        (tw_in, tw),
        (fb_in, fb),
        (gb_in, gb),
        (ga_in, ga),
        (gain_in, gain),
    )
    copies = [
        pltpu.make_async_copy(src, dst, table_sem.at[i]) for i, (src, dst) in enumerate(pairs)
    ]
    plane = n // 2
    here, spot = me // plane, lax.rem(me, plane)
    across = 1 - here

    depth = plane // RING
    far_first = sorted(
        ((dz, dx) for dz in range(depth) for dx in range(RING)),
        key=lambda offset: -min(offset[0], depth - offset[0]) - min(offset[1], RING - offset[1]),
    )

    def place_at(offset):
        dz, dx = offset
        return lax.rem(spot // RING + dz, depth) * RING + lax.rem(spot + dx, RING)

    barrier = pltpu.get_barrier_semaphore()

    def greet(place):
        pl.semaphore_signal(barrier, inc=1, device_id=place, device_id_type=MESH)

    for offset in far_first:
        greet({"seq": across * plane + place_at(offset)})
    for offset in far_first[:-1]:
        greet({"seq": here * plane + place_at(offset)})
    for partner in (mirror, corner, twin):
        greet({"chan": partner})
    for copy in copies:
        copy.start()

    def send(src, dst, phase, peer):
        pltpu.make_async_remote_copy(
            src_ref=src,
            dst_ref=dst,
            send_sem=send_sem.at[phase],
            recv_sem=recv_sem.at[phase],
            device_id={"seq": peer},
            device_id_type=MESH,
        ).start()

    def exchange(src, dst, phase, half, index, part):
        def at(ref, slot):
            return ref.at[slot, index, part]

        for offset in far_first:
            if half is here and offset == (0, 0):
                continue
            peer = half * plane + place_at(offset)
            send(at(src, peer), at(dst, me), phase, peer)
        if half is here:
            dst[me, index, part] = src[me, index, part]

    def exchange_all(src, dst, phase, index=0, part=slice(None)):
        exchange(src, dst, phase, across, index, part)
        exchange(src, dst, phase, here, index, part)

    def await_all(buf, sems, phase, count=n - 1, index=None):
        part = buf.at[pl.ds(0, count)] if index is None else buf.at[pl.ds(0, count), index]
        pltpu.make_async_copy(part, part, sems.at[phase]).wait()

    def turn(value, b):
        stage[pl.ds(b, LANES, stride=blocks), :] = value.T

    def pack(value, dst, index):
        for b in range(blocks):
            turn(value(b), b)
        put(dst, index)

    def put(dst, index):
        dst[:, index] = stage[...].astype(BF16).reshape(n, piece, LANES)

    def unpack(src, index):
        stage[...] = src[:, index].astype(F32).reshape(n * piece, LANES)
        return lambda b: stage[pl.ds(b, LANES, stride=blocks), :].T

    def block(ref, b):
        return ref[b * LANES : (b + 1) * LANES, :].astype(F32)

    def gather_part(src, buf, phase, k):
        size = positions // CHUNKS
        part = pl.ds(k * size, size)
        started = [
            pltpu.make_async_remote_copy(
                src_ref=src.at[part],
                dst_ref=buf.at[lane, part],
                send_sem=chan_send.at[phase, way, k],
                recv_sem=chan_recv.at[phase, way, k],
                device_id={"chan": partner},
                device_id_type=MESH,
            )
            for way, partner in enumerate((mirror, twin))
        ]
        for copy in started:
            copy.start()
        return started

    def relay(buf, phase, started, k):
        size = positions // CHUNKS
        part = pl.ds(k * size, size)
        started[k][0].wait_recv()
        passed = pltpu.make_async_remote_copy(
            src_ref=buf.at[mirror, part],
            dst_ref=buf.at[mirror, part],
            send_sem=relay_send.at[phase, k],
            recv_sem=relay_recv.at[phase, k],
            device_id={"chan": twin},
            device_id_type=MESH,
        )
        passed.start()
        return passed

    def forward(src, index, spec, pairs):
        for pair in pairs:
            x = src[:, index, 16 * pair : 16 * pair + 16, :].astype(F32)
            for half in range(2):
                xb[:, (2 * pair + half) * LANES : (2 * pair + half + 1) * LANES] = (
                    x[:, 8 * half : 8 * half + 8, :].reshape(rows, LANES).astype(BF16)
                )
            cols = xb[:, 2 * pair * LANES : (2 * pair + 2) * LANES]
            a = dot(fa[0], cols) + dot(fa[1], cols)
            for half in range(2):
                real = a[:rows, half * LANES : (half + 1) * LANES]
                imag = a[rows:, half * LANES : (half + 1) * LANES]
                c = 2 * pair + half
                t = jnp.concatenate(
                    [real * tw[0] - imag * tw[1], real * tw[1] + imag * tw[0]], axis=1
                )
                t_high[c * rows : (c + 1) * rows, :], t_low[c * rows : (c + 1) * rows, :] = split(t)
            for c in (2 * pair, 2 * pair + 1):
                part = slice(c * rows, (c + 1) * rows)
                spec[part, :] = (
                    dot(t_high[part, :], fb[0])
                    + dot(t_high[part, :], fb[1])
                    + dot(t_low[part, :], fb[0])
                )

    def inverse(left, right, conjugate, dst, index, pairs):
        sign = -1.0 if conjugate else 1.0
        for pair in pairs:
            for c in (2 * pair, 2 * pair + 1):
                part = slice(c * rows, (c + 1) * rows)
                l_real, l_imag = left[part, :LANES], sign * left[part, LANES:]
                r_real, r_imag = right[part, :LANES], right[part, LANES:]
                high, low = split(
                    jnp.concatenate(
                        [l_real * r_real - l_imag * r_imag, l_real * r_imag + l_imag * r_real],
                        axis=1,
                    )
                )
                y = dot(high, gb[0]) + dot(high, gb[1]) + dot(low, gb[0])
                real, imag = y[:, :LANES], y[:, LANES:]
                d_real = split(real * tw[0] + imag * tw[1])
                d_imag = split(imag * tw[0] - real * tw[1])
                cols = slice(c * LANES, (c + 1) * LANES)
                d_high[:rows, cols], d_low[:rows, cols] = d_real
                d_high[rows:, cols], d_low[rows:, cols] = d_imag
            cols = slice(2 * pair * LANES, (2 * pair + 2) * LANES)
            y = dot(ga[0], d_high[:, cols]) + dot(ga[1], d_high[:, cols]) + dot(ga[0], d_low[:, cols])
            dst[:, index, 16 * pair : 16 * pair + 16, :] = jnp.concatenate(
                [y[:, :LANES].reshape(n, 8, LANES), y[:, LANES:].reshape(n, 8, LANES)], axis=1
            ).astype(BF16)

    every = range(own // 2)

    team = min(8, plane)
    first_spot, rank = spot // team * team, lax.rem(spot, team)
    height = LANES // team
    mine = pl.ds(pl.multiple_of(rank * height, height), height)
    col_copies = []
    for k, partner in enumerate((mirror, corner, twin)):
        cols = pl.ds(pl.multiple_of(partner * LANES, LANES), LANES)
        part = mine if k < 2 else pl.ds(0, LANES)
        col_copies.append(
            pltpu.make_async_remote_copy(
                src_ref=weight.at[part, cols],
                dst_ref=columns.at[lane, part],
                send_sem=col_send.at[k],
                recv_sem=col_recv.at[k],
                device_id={"chan": partner},
                device_id_type=MESH,
            )
        )
    share = 4 * LANES // plane
    count = LANES // share
    held = {}

    def inner_out():
        exchange_all(first_send, first_recv, 0, 0)

    def taps_out():
        copies[2].wait()
        pack(lambda b: block(taps, b), first_send, 1)
        exchange_all(first_send, first_recv, 8, 1)

    def signals_left():
        await_all(first_send, send_sem, 0, index=0)
        await_all(first_send, send_sem, 8, index=1)

    def cot_out():
        held["cot"] += [gather_part(cot_in, cot_all, 0, k) for k in range(1, CHUNKS)]

    def cot_start():
        held["cot"] = [gather_part(cot_in, cot_all, 0, 0)]

    def columns_out():
        copies[4].wait()
        for copy in col_copies:
            copy.start()
        columns[lane] = weight[:, pl.ds(pl.multiple_of(lane * LANES, LANES), LANES)]

    def columns_on():
        for k, origin in enumerate((mirror, corner)):
            col_copies[k].wait_recv()
            part = columns.at[origin, mine]
            for step in range(1, team):
                peer = here * plane + first_spot + lax.rem(rank + step, team)
                send(part, part, 9 + k, peer)

    def cot_signal():
        copies[3].wait()
        copies[5].wait()
        held["cot_passed"] = []
        for k in range(CHUNKS + 1):
            if k < CHUNKS:
                held["cot_passed"].append(relay(cot_all, 0, held["cot"], k))
            if k == 0:
                continue
            held["cot"][k - 1][1].wait_recv()
            held["cot_passed"][k - 1].wait_recv()
            size = blocks // CHUNKS
            for b in range((k - 1) * size, k * size):
                part = pl.ds(b * LANES, LANES)
                total = jnp.zeros((LANES, LANES), F32)
                for g in range(0, 4, 2):
                    left = jnp.concatenate([cot_all[g, part], cot_all[g + 1, part]], axis=1)
                    total += lax.dot_general(
                        left,
                        weight[:, g * LANES : (g + 2) * LANES],
                        (((1,), (1,)), ((), ())),
                        preferred_element_type=F32,
                    )
                back[part, :] = total
                signal = total * block(queries, b)
                inner_cot[part, :] = signal
                turn(signal, b)
        put(cot_send, 0)
        exchange_all(cot_send, cot_recv, 1)

    def conv_signal():
        for copy in copies[6:]:
            copy.wait()
        await_all(first_recv, recv_sem, 0, index=0)
        forward(first_recv, 0, spec_inner, every)
        await_all(first_recv, recv_sem, 8, index=1)
        forward(first_recv, 1, spec_taps, every)
        inverse(spec_taps, spec_inner, False, conv_send, 0, every)
        exchange_all(conv_send, conv_recv, 2)

    def grad_signal():
        await_all(cot_recv, recv_sem, 1)
        forward(cot_recv, 0, spec_cot, every)
        inverse(spec_taps, spec_cot, True, grad_send, 0, every)

    def grad_out():
        exchange_all(grad_send, grad_recv, 3, 0)

    def taps_signal():
        inverse(spec_inner, spec_cot, True, grad_send, 1, every)

    def taps_grad_out():
        exchange_all(grad_send, grad_recv, 4, 1)

    def gate():
        await_all(conv_recv, recv_sem, 2)
        conv = unpack(conv_recv, 0)
        held["gated"] = []
        for b in range(blocks):
            part = pl.ds(b * LANES, LANES)
            mixed = conv(b) + gain[...] * (block(keys, b) * block(values, b))
            mixed_all[part, :] = mixed
            gated_all[lane, part, :] = (block(queries, b) * mixed).astype(BF16)
            if (b + 1) % (blocks // CHUNKS) == 0:
                k = b // (blocks // CHUNKS)
                held["gated"].append(gather_part(gated_all.at[lane], gated_all, 1, k))

    def skip_sum():
        skip = jnp.zeros((8, LANES), F32)
        for b in range(blocks):
            part = pl.ds(b * LANES, LANES)
            product = inner_cot[part, :] * (block(keys, b) * block(values, b))
            skip += jnp.sum(product.reshape(LANES // 8, 8, LANES), axis=0)
        high, low = split(skip)
        skip_recv[spot] = jnp.concatenate([high.astype(F32), low.astype(F32)], axis=0).astype(BF16)
        for offset in far_first[:-1]:
            send(skip_recv.at[spot], skip_recv.at[spot], 11, here * plane + place_at(offset))

    def query_grads():
        for b in range(blocks):
            part = pl.ds(b * LANES, LANES)
            query_o[part, :] = (back[part, :] * mixed_all[part, :]).astype(BF16)

    def weight_out():
        gated = gated_all[lane].T
        for g in range(4):
            term = dot(gated, cot_all[g]).astype(BF16)
            weight_send[g * count : (g + 1) * count] = term.reshape(count, share, LANES)

        for offset in far_first[:-1]:
            place = place_at(offset)
            send(weight_send.at[place], weight_recv.at[spot], 5, here * plane + place)
        weight_recv[spot] = weight_send[spot]

    def weight_pair():
        await_all(weight_recv, recv_sem, 5, plane - 1)
        pair_send[:share, :] = jnp.sum(weight_recv[...].astype(F32), axis=0)
        await_all(skip_recv, recv_sem, 11, plane - 1)
        skip = jnp.sum(skip_recv[...].astype(F32), axis=0)
        pair_send[share:, :] = skip[:8] + skip[8:]
        send(pair_send, pair_recv, 6, across * plane + spot)

    def weight_total():
        pltpu.make_async_copy(pair_recv, pair_recv, recv_sem.at[6]).wait()
        sums = pair_send[...] + pair_recv[...]
        total_recv[spot] = sums[:share].astype(BF16)
        skip_o[...] = jnp.sum(sums[share:], axis=0, keepdims=True) * scale

        for offset in far_first[:-1]:
            send(total_recv.at[spot], total_recv.at[spot], 7, here * plane + place_at(offset))

    def gated_relay():
        held["gated_passed"] = [relay(gated_all, 1, held["gated"], k) for k in range(CHUNKS)]

    def project():
        for copy in [pair[1] for pair in held["gated"]] + held["gated_passed"] + col_copies[2:]:
            copy.wait_recv()
        others = columns.at[0, pl.ds(0, LANES - height)]
        for phase in (9, 10):
            pltpu.make_async_copy(others, others, recv_sem.at[phase]).wait()
        half = positions // 2
        for k in range(2):
            part = pl.ds(k * half, half)
            total = jnp.zeros((half, LANES), F32)
            for g in range(0, 4, 2):
                left = jnp.concatenate([gated_all[g, part], gated_all[g + 1, part]], axis=1)
                total += dot(left, columns[g : g + 2].reshape(2 * LANES, LANES))
            out_o[part, :] = total.astype(BF16)

    def factor_grads():
        await_all(grad_recv, recv_sem, 3, index=0)
        grad = unpack(grad_recv, 0)
        for b in range(blocks):
            part = pl.ds(b * LANES, LANES)
            inner_grad = grad(b) + gain[...] * inner_cot[part, :]
            key_o[part, :] = (inner_grad * block(values, b)).astype(BF16)
            value_o[part, :] = (inner_grad * block(keys, b)).astype(BF16)

    def settle():
        await_all(grad_recv, recv_sem, 4, index=1)
        await_all(total_recv, recv_sem, 7, plane - 1)
        await_all(cot_send, send_sem, 1)
        await_all(conv_send, send_sem, 2)
        await_all(grad_send, send_sem, 3, index=0)
        await_all(grad_send, send_sem, 4, index=1)
        await_all(weight_send, send_sem, 5, plane - 1)
        await_all(skip_recv, send_sem, 11, plane - 1)
        pltpu.make_async_copy(pair_send, pair_send, send_sem.at[6]).wait()
        await_all(total_recv, send_sem, 7, plane - 1)
        for name in ("cot", "gated"):
            for copy in sum(held[name], held[name + "_passed"]):
                copy.wait_send()
        others = columns.at[0, pl.ds(0, LANES - height)]
        for phase in (9, 10):
            pltpu.make_async_copy(others, others, send_sem.at[phase]).wait()
        for copy in col_copies:
            copy.wait_send()

    copies[0].wait()
    copies[1].wait()
    pack(lambda b: block(keys, b) * block(values, b), first_send, 0)
    pl.semaphore_wait(barrier, n + 2)
    for step in (
        cot_start,
        inner_out,
        taps_out,
        cot_out,
        conv_signal,
        columns_out,
        cot_signal,
        skip_sum,
        gate,
        weight_out,
        columns_on,
        grad_signal,
        weight_pair,
        grad_out,
        taps_signal,
        weight_total,
        taps_grad_out,
        query_grads,
        gated_relay,
        signals_left,
        project,
        factor_grads,
        settle,
    ):
        step()


def store(scale, *refs):
    sources, places, (stage, weights, taps, sems) = list(refs[:7]), refs[7:14], refs[14:]
    (total, grad), sources[4:6] = sources[4:6], (weights, taps)
    copies = [
        pltpu.make_async_copy(src, dst, sems.at[i])
        for i, (src, dst) in enumerate(zip(sources, places))
    ]
    for copy in copies[:4] + copies[6:]:
        copy.start()
    positions = taps.shape[0]
    blocks = positions // LANES
    stage[...] = grad[:, 1].astype(F32).reshape(positions, LANES)
    for b in range(blocks):
        taps[pl.ds(b * LANES, LANES), :] = stage[pl.ds(b, LANES, stride=blocks), :].T * scale
    copies[5].start()
    count = total.shape[0] // 4
    for g in range(4):
        weights[:, g * LANES : (g + 1) * LANES] = (
            total[g * count : (g + 1) * count].astype(F32).reshape(LANES, LANES) * scale
        )
    copies[4].start()
    for copy in copies:
        copy.wait()


def local(n, queries, keys, values, cotangent, out_weight, taps, skip_gain):
    positions = keys.shape[0]
    blocks = positions // LANES
    rows = n * blocks
    own = LANES // n
    piece = own * blocks
    plane = n // 2
    share = 4 * LANES // plane
    vmem = pl.BlockSpec(memory_space=pltpu.VMEM)
    far = pl.BlockSpec(memory_space=pltpu.HBM)
    wide = jax.ShapeDtypeStruct((positions, LANES), BF16)
    wide_f32 = jax.ShapeDtypeStruct((positions, LANES), F32)
    square = jax.ShapeDtypeStruct((LANES, 4 * LANES), F32)
    line = jax.ShapeDtypeStruct((1, LANES), F32)
    gain = skip_gain.reshape(1, LANES)

    def buffer(count):
        return pltpu.VMEM((n, count, piece, LANES), BF16)

    shapes = [wide, wide, wide, wide, square, wide_f32, line]
    results = pl.pallas_call(
        functools.partial(kernel, n),
        out_shape=[
            *shapes[:4],
            jax.ShapeDtypeStruct((plane, share, LANES), BF16),
            jax.ShapeDtypeStruct((n, 2, piece, LANES), BF16),
            line,
        ],
        in_specs=[far] * 12,
        out_specs=[vmem] * 7,
        scratch_shapes=[
            pltpu.VMEM((positions, LANES), F32),
            pltpu.VMEM((positions, LANES), BF16),
            pltpu.VMEM((positions, LANES), BF16),
            pltpu.VMEM((positions, LANES), F32),
            pltpu.VMEM((4, positions, LANES), BF16),
            pltpu.VMEM((LANES, 4 * LANES), BF16),
            pltpu.VMEM((positions, LANES), BF16),
            pltpu.VMEM((2, 2 * rows, rows), BF16),
            pltpu.VMEM((2, rows, LANES), F32),
            pltpu.VMEM((2, 2 * LANES, 2 * LANES), BF16),
            pltpu.VMEM((2, 2 * LANES, 2 * LANES), BF16),
            pltpu.VMEM((2, rows, 2 * rows), BF16),
            pltpu.VMEM((1, LANES), F32),
            pltpu.VMEM((positions, LANES), F32),
            buffer(2),
            buffer(2),
            buffer(1),
            buffer(1),
            buffer(1),
            buffer(1),
            buffer(2),
            pltpu.VMEM((plane, 16, LANES), BF16),
            pltpu.VMEM((plane, share, LANES), BF16),
            pltpu.VMEM((plane, share, LANES), BF16),
            pltpu.VMEM((share + 8, LANES), F32),
            pltpu.VMEM((share + 8, LANES), F32),
            pltpu.VMEM((4, positions, LANES), BF16),
            pltpu.VMEM((4, LANES, LANES), BF16),
            pltpu.VMEM((positions, LANES), F32),
            pltpu.VMEM((positions, LANES), F32),
            pltpu.VMEM((rows, own * LANES), BF16),
            pltpu.VMEM((own * rows, 2 * LANES), BF16),
            pltpu.VMEM((own * rows, 2 * LANES), BF16),
            pltpu.VMEM((2 * rows, own * LANES), BF16),
            pltpu.VMEM((2 * rows, own * LANES), BF16),
            pltpu.VMEM((own * rows, 2 * LANES), F32),
            pltpu.VMEM((own * rows, 2 * LANES), F32),
            pltpu.VMEM((own * rows, 2 * LANES), F32),
            pltpu.SemaphoreType.DMA((12,)),
            pltpu.SemaphoreType.DMA((12,)),
            pltpu.SemaphoreType.DMA((12,)),
            pltpu.SemaphoreType.DMA((2, 2, CHUNKS)),
            pltpu.SemaphoreType.DMA((2, 2, CHUNKS)),
            pltpu.SemaphoreType.DMA((2, CHUNKS)),
            pltpu.SemaphoreType.DMA((2, CHUNKS)),
            pltpu.SemaphoreType.DMA((3,)),
            pltpu.SemaphoreType.DMA((3,)),
        ],
        compiler_params=pltpu.CompilerParams(
            collective_id=0, has_side_effects=True, vmem_limit_bytes=40 * 1024 * 1024
        ),
        name="hyena",
    )(*map(in_hbm, (keys, values, taps, cotangent, out_weight, queries, *tables(rows), gain)))
    outs = pl.pallas_call(
        functools.partial(store, 1.0 / math.sqrt(positions * n)),
        out_shape=shapes,
        in_specs=[vmem] * 7,
        out_specs=[far] * 7,
        scratch_shapes=[
            pltpu.VMEM((positions, LANES), F32),
            pltpu.VMEM((LANES, 4 * LANES), F32),
            pltpu.VMEM((positions, LANES), F32),
            pltpu.SemaphoreType.DMA((7,)),
        ],
        compiler_params=pltpu.CompilerParams(vmem_limit_bytes=16 * 1024 * 1024),
        name="store",
    )(*results)
    return (*outs[:6], outs[6].reshape(LANES))


def solution(mesh):
    wide = P("seq", "chan")
    return jax.shard_map(
        functools.partial(local, mesh.shape["seq"]),
        mesh=mesh,
        in_specs=(wide, wide, wide, wide, P("chan", None), wide, P("chan")),
        out_specs=(wide, wide, wide, wide, P("chan", None), wide, P("chan")),
        check_vma=False,
    )
```

```python
import functools
import math

import jax
import jax.numpy as jnp
import numpy as np
from jax import lax
from jax.experimental import pallas as pl
from jax.experimental.pallas import tpu as pltpu
from jax.sharding import PartitionSpec as P

MESH = pl.DeviceIdType.MESH
BF16 = jnp.bfloat16
F32 = jnp.float32
LANES = 128
PARTS = ((2, 3, 3), (4, 4))
RING = 4


def split_table(table):
    high = table.astype(BF16)
    low = (table - high.astype(np.float64)).astype(BF16)
    return jnp.asarray(np.stack([high, low]))


def tables(rows):
    count = rows * LANES
    ids = np.arange(rows)
    lane = np.arange(LANES)
    first = 2.0 * np.pi * (((4 * ids[:, None] + 1) * ids[None, :]) % (4 * rows)) / (4 * rows)
    second = 2.0 * np.pi * ((lane[:, None] * lane[None, :]) % LANES) / LANES
    twist = 2.0 * np.pi * ((4 * ids[:, None] + 1) * lane[None, :]) / (4 * count)
    cos, sin = np.cos(second), np.sin(second)
    return (
        split_table(np.concatenate([np.cos(first), np.sin(first)], axis=0)),
        jnp.asarray(np.stack([np.cos(twist), np.sin(twist)]), F32),
        split_table(np.block([[cos, sin], [-sin, cos]])),
        split_table(np.block([[cos, -sin], [sin, cos]])),
        split_table(np.concatenate([np.cos(first).T, np.sin(first).T], axis=1) / count),
    )


def in_hbm(array):
    return pltpu.with_memory_space_constraint(array, pltpu.HBM)


def dot(left, right):
    return jnp.dot(left, right, preferred_element_type=F32)


def split(value):
    high = value.astype(BF16)
    return high, (value - high.astype(F32)).astype(BF16)


def kernel(
    n,
    keys_in,
    values_in,
    taps_in,
    cot_in,
    weight_in,
    queries_in,
    fa_in,
    tw_in,
    fb_in,
    gb_in,
    ga_in,
    gain_in,
    out_o,
    query_o,
    key_o,
    value_o,
    total_recv,
    grad_recv,
    skip_o,
    inner_cot,
    keys,
    values,
    taps,
    cot_all,
    weight,
    queries,
    fa,
    tw,
    fb,
    gb,
    ga,
    gain,
    stage,
    first_send,
    first_recv,
    cot_send,
    cot_recv,
    conv_send,
    conv_recv,
    grad_send,
    skip_recv,
    weight_send,
    weight_recv,
    pair_send,
    pair_recv,
    gated_all,
    columns,
    back,
    mixed_all,
    xb,
    t_high,
    t_low,
    d_high,
    d_low,
    spec_inner,
    spec_taps,
    spec_cot,
    table_sem,
    send_sem,
    recv_sem,
    chan_send,
    chan_recv,
    relay_send,
    relay_recv,
    col_send,
    col_recv,
):
    me = lax.axis_index("seq")
    lane = lax.axis_index("chan")
    core, chip = lax.rem(lane, 2), lane // 2
    twin = 2 * chip + 1 - core
    mirror = 2 * (1 - chip) + core
    corner = 2 * (1 - chip) + 1 - core
    positions = keys.shape[0]
    blocks = positions // LANES
    rows = n * blocks
    own = LANES // n
    piece = own * blocks
    window = positions * n
    scale = 1.0 / math.sqrt(window)

    pairs = (
        (keys_in, keys),
        (values_in, values),
        (taps_in, taps),
        (cot_in, cot_all.at[lane]),
        (weight_in, weight),
        (queries_in, queries),
        (fa_in, fa),
        (tw_in, tw),
        (fb_in, fb),
        (gb_in, gb),
        (ga_in, ga),
        (gain_in, gain),
    )
    copies = [
        pltpu.make_async_copy(src, dst, table_sem.at[i]) for i, (src, dst) in enumerate(pairs)
    ]
    plane = n // 2
    here, spot = me // plane, lax.rem(me, plane)
    across = 1 - here

    depth = plane // RING
    far_first = sorted(
        ((dz, dx) for dz in range(depth) for dx in range(RING)),
        key=lambda offset: -min(offset[0], depth - offset[0]) - min(offset[1], RING - offset[1]),
    )

    def place_at(offset):
        dz, dx = offset
        return lax.rem(spot // RING + dz, depth) * RING + lax.rem(spot + dx, RING)

    barrier = pltpu.get_barrier_semaphore()

    def greet(place):
        pl.semaphore_signal(barrier, inc=1, device_id=place, device_id_type=MESH)

    for offset in far_first:
        greet({"seq": across * plane + place_at(offset)})
    for offset in far_first[:-1]:
        greet({"seq": here * plane + place_at(offset)})
    for partner in (mirror, corner, twin):
        greet({"chan": partner})
    for copy in copies:
        copy.start()

    def send(src, dst, phase, peer):
        pltpu.make_async_remote_copy(
            src_ref=src,
            dst_ref=dst,
            send_sem=send_sem.at[phase],
            recv_sem=recv_sem.at[phase],
            device_id={"seq": peer},
            device_id_type=MESH,
        ).start()

    def exchange(src, dst, phase, half, index, part):
        def at(ref, slot):
            return ref.at[slot, index, part]

        for offset in far_first:
            if half is here and offset == (0, 0):
                continue
            peer = half * plane + place_at(offset)
            send(at(src, peer), at(dst, me), phase, peer)
        if half is here:
            dst[me, index, part] = src[me, index, part]

    def exchange_all(src, dst, phase, index=0, part=slice(None)):
        exchange(src, dst, phase, across, index, part)
        exchange(src, dst, phase, here, index, part)

    def await_all(buf, sems, phase, count=n - 1, index=None):
        part = buf.at[pl.ds(0, count)] if index is None else buf.at[pl.ds(0, count), index]
        pltpu.make_async_copy(part, part, sems.at[phase]).wait()

    def turn(value, b):
        stage[pl.ds(b, LANES, stride=blocks), :] = value.T

    def pack(value, dst, index):
        for b in range(blocks):
            turn(value(b), b)
        put(dst, index)

    def put(dst, index):
        dst[:, index] = stage[...].astype(BF16).reshape(n, piece, LANES)

    def unpack(src, index):
        stage[...] = src[:, index].astype(F32).reshape(n * piece, LANES)
        return lambda b: stage[pl.ds(b, LANES, stride=blocks), :].T

    def block(ref, b):
        return ref[b * LANES : (b + 1) * LANES, :].astype(F32)

    def gather_part(src, buf, phase, k):
        part = pl.ds(sum(PARTS[phase][:k]) * LANES, PARTS[phase][k] * LANES)
        started = [
            pltpu.make_async_remote_copy(
                src_ref=src.at[part],
                dst_ref=buf.at[lane, part],
                send_sem=chan_send.at[phase, way, k],
                recv_sem=chan_recv.at[phase, way, k],
                device_id={"chan": partner},
                device_id_type=MESH,
            )
            for way, partner in enumerate((mirror, twin))
        ]
        for copy in started:
            copy.start()
        return started

    def relay(buf, phase, started, k):
        part = pl.ds(sum(PARTS[phase][:k]) * LANES, PARTS[phase][k] * LANES)
        started[k][0].wait_recv()
        passed = pltpu.make_async_remote_copy(
            src_ref=buf.at[mirror, part],
            dst_ref=buf.at[mirror, part],
            send_sem=relay_send.at[phase, k],
            recv_sem=relay_recv.at[phase, k],
            device_id={"chan": twin},
            device_id_type=MESH,
        )
        passed.start()
        return passed

    def forward(src, index, spec, pairs):
        for pair in pairs:
            x = src[:, index, 16 * pair : 16 * pair + 16, :].astype(F32)
            for half in range(2):
                xb[:, (2 * pair + half) * LANES : (2 * pair + half + 1) * LANES] = (
                    x[:, 8 * half : 8 * half + 8, :].reshape(rows, LANES).astype(BF16)
                )
            cols = xb[:, 2 * pair * LANES : (2 * pair + 2) * LANES]
            a = dot(fa[0], cols) + dot(fa[1], cols)
            for half in range(2):
                real = a[:rows, half * LANES : (half + 1) * LANES]
                imag = a[rows:, half * LANES : (half + 1) * LANES]
                c = 2 * pair + half
                t = jnp.concatenate(
                    [real * tw[0] - imag * tw[1], real * tw[1] + imag * tw[0]], axis=1
                )
                t_high[c * rows : (c + 1) * rows, :], t_low[c * rows : (c + 1) * rows, :] = split(t)
            for c in (2 * pair, 2 * pair + 1):
                part = slice(c * rows, (c + 1) * rows)
                spec[part, :] = (
                    dot(t_high[part, :], fb[0])
                    + dot(t_high[part, :], fb[1])
                    + dot(t_low[part, :], fb[0])
                )

    def inverse(left, right, conjugate, dst, index, pairs):
        sign = -1.0 if conjugate else 1.0
        for pair in pairs:
            for c in (2 * pair, 2 * pair + 1):
                part = slice(c * rows, (c + 1) * rows)
                l_real, l_imag = left[part, :LANES], sign * left[part, LANES:]
                r_real, r_imag = right[part, :LANES], right[part, LANES:]
                high, low = split(
                    jnp.concatenate(
                        [l_real * r_real - l_imag * r_imag, l_real * r_imag + l_imag * r_real],
                        axis=1,
                    )
                )
                y = dot(high, gb[0]) + dot(high, gb[1]) + dot(low, gb[0])
                real, imag = y[:, :LANES], y[:, LANES:]
                d_real = split(real * tw[0] + imag * tw[1])
                d_imag = split(imag * tw[0] - real * tw[1])
                cols = slice(c * LANES, (c + 1) * LANES)
                d_high[:rows, cols], d_low[:rows, cols] = d_real
                d_high[rows:, cols], d_low[rows:, cols] = d_imag
            cols = slice(2 * pair * LANES, (2 * pair + 2) * LANES)
            y = dot(ga[0], d_high[:, cols]) + dot(ga[1], d_high[:, cols]) + dot(ga[0], d_low[:, cols])
            dst[:, index, 16 * pair : 16 * pair + 16, :] = jnp.concatenate(
                [y[:, :LANES].reshape(n, 8, LANES), y[:, LANES:].reshape(n, 8, LANES)], axis=1
            ).astype(BF16)

    every = range(own // 2)

    team = min(8, plane)
    first_spot, rank = spot // team * team, lax.rem(spot, team)
    height = LANES // team
    mine = pl.ds(pl.multiple_of(rank * height, height), height)
    col_copies = []
    for k, partner in enumerate((mirror, corner, twin)):
        cols = pl.ds(pl.multiple_of(partner * LANES, LANES), LANES)
        part = mine if k < 2 else pl.ds(0, LANES)
        col_copies.append(
            pltpu.make_async_remote_copy(
                src_ref=weight.at[part, cols],
                dst_ref=columns.at[lane, part],
                send_sem=col_send.at[k],
                recv_sem=col_recv.at[k],
                device_id={"chan": partner},
                device_id_type=MESH,
            )
        )
    share = 4 * LANES // plane
    count = LANES // share
    held = {}

    def inner_out():
        exchange_all(first_send, first_recv, 0, 0)

    def taps_out():
        copies[2].wait()
        pack(lambda b: block(taps, b), first_send, 1)
        exchange_all(first_send, first_recv, 8, 1)

    def signals_left():
        await_all(first_send, send_sem, 0, index=0)
        await_all(first_send, send_sem, 8, index=1)

    def cot_out():
        held["cot"] += [gather_part(cot_in, cot_all, 0, k) for k in range(1, len(PARTS[0]))]

    def cot_start():
        held["cot"] = [gather_part(cot_in, cot_all, 0, 0)]

    def columns_out():
        copies[4].wait()
        for copy in col_copies:
            copy.start()
        columns[lane] = weight[:, pl.ds(pl.multiple_of(lane * LANES, LANES), LANES)]

    def columns_on():
        for k, origin in enumerate((mirror, corner)):
            col_copies[k].wait_recv()
            part = columns.at[origin, mine]
            for step in range(1, team):
                peer = here * plane + first_spot + lax.rem(rank + step, team)
                send(part, part, 9 + k, peer)

    def cot_signal():
        copies[3].wait()
        copies[5].wait()
        held["cot_passed"] = []
        for k in range(len(PARTS[0]) + 1):
            if k < len(PARTS[0]):
                held["cot_passed"].append(relay(cot_all, 0, held["cot"], k))
            if k == 0:
                continue
            held["cot"][k - 1][1].wait_recv()
            held["cot_passed"][k - 1].wait_recv()
            for b in range(sum(PARTS[0][: k - 1]), sum(PARTS[0][:k])):
                part = pl.ds(b * LANES, LANES)
                total = jnp.zeros((LANES, LANES), F32)
                for g in range(0, 4, 2):
                    left = jnp.concatenate([cot_all[g, part], cot_all[g + 1, part]], axis=1)
                    total += lax.dot_general(
                        left,
                        weight[:, g * LANES : (g + 2) * LANES],
                        (((1,), (1,)), ((), ())),
                        preferred_element_type=F32,
                    )
                back[part, :] = total
                signal = total * block(queries, b)
                inner_cot[part, :] = signal
                turn(signal, b)
        put(cot_send, 0)
        exchange_all(cot_send, cot_recv, 1)

    def conv_signal():
        for copy in copies[6:]:
            copy.wait()
        await_all(first_recv, recv_sem, 0, index=0)
        forward(first_recv, 0, spec_inner, every)
        await_all(first_recv, recv_sem, 8, index=1)
        forward(first_recv, 1, spec_taps, every)
        inverse(spec_taps, spec_inner, False, conv_send, 0, every)
        exchange_all(conv_send, conv_recv, 2)

    def grad_signal():
        await_all(cot_recv, recv_sem, 1)
        forward(cot_recv, 0, spec_cot, every)
        inverse(spec_taps, spec_cot, True, grad_send, 0, every)

    def grad_out():
        exchange_all(grad_send, grad_recv, 3, 0)

    def taps_signal():
        inverse(spec_inner, spec_cot, True, grad_send, 1, every)

    def taps_grad_out():
        exchange_all(grad_send, grad_recv, 4, 1)

    def gate():
        await_all(conv_recv, recv_sem, 2)
        conv = unpack(conv_recv, 0)
        held["gated"] = []
        for b in range(blocks):
            part = pl.ds(b * LANES, LANES)
            mixed = conv(b) + gain[...] * (block(keys, b) * block(values, b))
            mixed_all[part, :] = mixed
            gated_all[lane, part, :] = (block(queries, b) * mixed).astype(BF16)
            k = len(held["gated"])
            if b + 1 == sum(PARTS[1][: k + 1]):
                held["gated"].append(gather_part(gated_all.at[lane], gated_all, 1, k))

    def skip_sum():
        skip = jnp.zeros((8, LANES), F32)
        for b in range(blocks):
            part = pl.ds(b * LANES, LANES)
            product = inner_cot[part, :] * (block(keys, b) * block(values, b))
            skip += jnp.sum(product.reshape(LANES // 8, 8, LANES), axis=0)
        high, low = split(skip)
        skip_recv[spot] = jnp.concatenate([high.astype(F32), low.astype(F32)], axis=0).astype(BF16)
        for offset in far_first[:-1]:
            send(skip_recv.at[spot], skip_recv.at[spot], 11, here * plane + place_at(offset))

    def query_grads():
        for b in range(blocks):
            part = pl.ds(b * LANES, LANES)
            query_o[part, :] = (back[part, :] * mixed_all[part, :]).astype(BF16)

    def weight_out():
        gated = gated_all[lane].T
        for g in range(4):
            term = dot(gated, cot_all[g]).astype(BF16)
            weight_send[g * count : (g + 1) * count] = term.reshape(count, share, LANES)

        for offset in far_first[:-1]:
            place = place_at(offset)
            send(weight_send.at[place], weight_recv.at[spot], 5, here * plane + place)
        weight_recv[spot] = weight_send[spot]

    def weight_pair():
        await_all(weight_recv, recv_sem, 5, plane - 1)
        pair_send[:share, :] = jnp.sum(weight_recv[...].astype(F32), axis=0)
        await_all(skip_recv, recv_sem, 11, plane - 1)
        skip = jnp.sum(skip_recv[...].astype(F32), axis=0)
        pair_send[share:, :] = skip[:8] + skip[8:]
        send(pair_send, pair_recv, 6, across * plane + spot)

    def weight_total():
        pltpu.make_async_copy(pair_recv, pair_recv, recv_sem.at[6]).wait()
        sums = pair_send[...] + pair_recv[...]
        total_recv[spot] = sums[:share].astype(BF16)
        skip_o[...] = jnp.sum(sums[share:], axis=0, keepdims=True) * scale

        for offset in far_first[:-1]:
            send(total_recv.at[spot], total_recv.at[spot], 7, here * plane + place_at(offset))

    def gated_relay():
        held["gated_passed"] = [
            relay(gated_all, 1, held["gated"], k) for k in range(len(PARTS[1]))
        ]

    def project():
        for copy in [pair[1] for pair in held["gated"]] + held["gated_passed"] + col_copies[2:]:
            copy.wait_recv()
        others = columns.at[0, pl.ds(0, LANES - height)]
        for phase in (9, 10):
            pltpu.make_async_copy(others, others, recv_sem.at[phase]).wait()
        half = positions // 2
        for k in range(2):
            part = pl.ds(k * half, half)
            total = jnp.zeros((half, LANES), F32)
            for g in range(0, 4, 2):
                left = jnp.concatenate([gated_all[g, part], gated_all[g + 1, part]], axis=1)
                total += dot(left, columns[g : g + 2].reshape(2 * LANES, LANES))
            out_o[part, :] = total.astype(BF16)

    def factor_grads():
        await_all(grad_recv, recv_sem, 3, index=0)
        grad = unpack(grad_recv, 0)
        for b in range(blocks):
            part = pl.ds(b * LANES, LANES)
            inner_grad = grad(b) + gain[...] * inner_cot[part, :]
            key_o[part, :] = (inner_grad * block(values, b)).astype(BF16)
            value_o[part, :] = (inner_grad * block(keys, b)).astype(BF16)

    def settle():
        await_all(grad_recv, recv_sem, 4, index=1)
        await_all(total_recv, recv_sem, 7, plane - 1)
        await_all(cot_send, send_sem, 1)
        await_all(conv_send, send_sem, 2)
        await_all(grad_send, send_sem, 3, index=0)
        await_all(grad_send, send_sem, 4, index=1)
        await_all(weight_send, send_sem, 5, plane - 1)
        await_all(skip_recv, send_sem, 11, plane - 1)
        pltpu.make_async_copy(pair_send, pair_send, send_sem.at[6]).wait()
        await_all(total_recv, send_sem, 7, plane - 1)
        for name in ("cot", "gated"):
            for copy in sum(held[name], held[name + "_passed"]):
                copy.wait_send()
        others = columns.at[0, pl.ds(0, LANES - height)]
        for phase in (9, 10):
            pltpu.make_async_copy(others, others, send_sem.at[phase]).wait()
        for copy in col_copies:
            copy.wait_send()

    copies[0].wait()
    copies[1].wait()
    pack(lambda b: block(keys, b) * block(values, b), first_send, 0)
    pl.semaphore_wait(barrier, n + 2)
    for step in (
        cot_start,
        inner_out,
        taps_out,
        cot_out,
        conv_signal,
        columns_out,
        cot_signal,
        skip_sum,
        gate,
        weight_out,
        columns_on,
        grad_signal,
        weight_pair,
        grad_out,
        taps_signal,
        weight_total,
        taps_grad_out,
        query_grads,
        gated_relay,
        signals_left,
        project,
        factor_grads,
        settle,
    ):
        step()


def store(scale, *refs):
    sources, places, (stage, weights, taps, sems) = list(refs[:7]), refs[7:14], refs[14:]
    (total, grad), sources[4:6] = sources[4:6], (weights, taps)
    copies = [
        pltpu.make_async_copy(src, dst, sems.at[i])
        for i, (src, dst) in enumerate(zip(sources, places))
    ]
    for copy in copies[:4] + copies[6:]:
        copy.start()
    positions = taps.shape[0]
    blocks = positions // LANES
    stage[...] = grad[:, 1].astype(F32).reshape(positions, LANES)
    for b in range(blocks):
        taps[pl.ds(b * LANES, LANES), :] = stage[pl.ds(b, LANES, stride=blocks), :].T * scale
    copies[5].start()
    count = total.shape[0] // 4
    for g in range(4):
        weights[:, g * LANES : (g + 1) * LANES] = (
            total[g * count : (g + 1) * count].astype(F32).reshape(LANES, LANES) * scale
        )
    copies[4].start()
    for copy in copies:
        copy.wait()


def local(n, queries, keys, values, cotangent, out_weight, taps, skip_gain):
    positions = keys.shape[0]
    blocks = positions // LANES
    rows = n * blocks
    own = LANES // n
    piece = own * blocks
    plane = n // 2
    share = 4 * LANES // plane
    vmem = pl.BlockSpec(memory_space=pltpu.VMEM)
    far = pl.BlockSpec(memory_space=pltpu.HBM)
    wide = jax.ShapeDtypeStruct((positions, LANES), BF16)
    wide_f32 = jax.ShapeDtypeStruct((positions, LANES), F32)
    square = jax.ShapeDtypeStruct((LANES, 4 * LANES), F32)
    line = jax.ShapeDtypeStruct((1, LANES), F32)
    gain = skip_gain.reshape(1, LANES)

    def buffer(count):
        return pltpu.VMEM((n, count, piece, LANES), BF16)

    shapes = [wide, wide, wide, wide, square, wide_f32, line]
    results = pl.pallas_call(
        functools.partial(kernel, n),
        out_shape=[
            *shapes[:4],
            jax.ShapeDtypeStruct((plane, share, LANES), BF16),
            jax.ShapeDtypeStruct((n, 2, piece, LANES), BF16),
            line,
        ],
        in_specs=[far] * 12,
        out_specs=[vmem] * 7,
        scratch_shapes=[
            pltpu.VMEM((positions, LANES), F32),
            pltpu.VMEM((positions, LANES), BF16),
            pltpu.VMEM((positions, LANES), BF16),
            pltpu.VMEM((positions, LANES), F32),
            pltpu.VMEM((4, positions, LANES), BF16),
            pltpu.VMEM((LANES, 4 * LANES), BF16),
            pltpu.VMEM((positions, LANES), BF16),
            pltpu.VMEM((2, 2 * rows, rows), BF16),
            pltpu.VMEM((2, rows, LANES), F32),
            pltpu.VMEM((2, 2 * LANES, 2 * LANES), BF16),
            pltpu.VMEM((2, 2 * LANES, 2 * LANES), BF16),
            pltpu.VMEM((2, rows, 2 * rows), BF16),
            pltpu.VMEM((1, LANES), F32),
            pltpu.VMEM((positions, LANES), F32),
            buffer(2),
            buffer(2),
            buffer(1),
            buffer(1),
            buffer(1),
            buffer(1),
            buffer(2),
            pltpu.VMEM((plane, 16, LANES), BF16),
            pltpu.VMEM((plane, share, LANES), BF16),
            pltpu.VMEM((plane, share, LANES), BF16),
            pltpu.VMEM((share + 8, LANES), F32),
            pltpu.VMEM((share + 8, LANES), F32),
            pltpu.VMEM((4, positions, LANES), BF16),
            pltpu.VMEM((4, LANES, LANES), BF16),
            pltpu.VMEM((positions, LANES), F32),
            pltpu.VMEM((positions, LANES), F32),
            pltpu.VMEM((rows, own * LANES), BF16),
            pltpu.VMEM((own * rows, 2 * LANES), BF16),
            pltpu.VMEM((own * rows, 2 * LANES), BF16),
            pltpu.VMEM((2 * rows, own * LANES), BF16),
            pltpu.VMEM((2 * rows, own * LANES), BF16),
            pltpu.VMEM((own * rows, 2 * LANES), F32),
            pltpu.VMEM((own * rows, 2 * LANES), F32),
            pltpu.VMEM((own * rows, 2 * LANES), F32),
            pltpu.SemaphoreType.DMA((12,)),
            pltpu.SemaphoreType.DMA((12,)),
            pltpu.SemaphoreType.DMA((12,)),
            pltpu.SemaphoreType.DMA((2, 2, max(map(len, PARTS)))),
            pltpu.SemaphoreType.DMA((2, 2, max(map(len, PARTS)))),
            pltpu.SemaphoreType.DMA((2, max(map(len, PARTS)))),
            pltpu.SemaphoreType.DMA((2, max(map(len, PARTS)))),
            pltpu.SemaphoreType.DMA((3,)),
            pltpu.SemaphoreType.DMA((3,)),
        ],
        compiler_params=pltpu.CompilerParams(
            collective_id=0, has_side_effects=True, vmem_limit_bytes=40 * 1024 * 1024
        ),
        name="hyena",
    )(*map(in_hbm, (keys, values, taps, cotangent, out_weight, queries, *tables(rows), gain)))
    outs = pl.pallas_call(
        functools.partial(store, 1.0 / math.sqrt(positions * n)),
        out_shape=shapes,
        in_specs=[vmem] * 7,
        out_specs=[far] * 7,
        scratch_shapes=[
            pltpu.VMEM((positions, LANES), F32),
            pltpu.VMEM((LANES, 4 * LANES), F32),
            pltpu.VMEM((positions, LANES), F32),
            pltpu.SemaphoreType.DMA((7,)),
        ],
        compiler_params=pltpu.CompilerParams(vmem_limit_bytes=16 * 1024 * 1024),
        name="store",
    )(*results)
    return (*outs[:6], outs[6].reshape(LANES))


def solution(mesh):
    wide = P("seq", "chan")
    return jax.shard_map(
        functools.partial(local, mesh.shape["seq"]),
        mesh=mesh,
        in_specs=(wide, wide, wide, wide, P("chan", None), wide, P("chan")),
        out_specs=(wide, wide, wide, wide, P("chan", None), wide, P("chan")),
        check_vma=False,
    )
```
